512 devices in a mesh: pair: 128 (over y, z, core), red: 4 (over x).
Axes of the slice: x: 4, y: 4, z: 16, core: 2. Of those that a mesh axis runs over, the one named last changes fastest.
Arguments:
- amplitudes: bfloat16 [2048, 4096], P('pair', 'red'), may hold values from -6 to 6
- integrals: bfloat16 [4096, 65536], P('red', 'pair'), may hold values from -0.125 to 0.125
- pattern: int32 [128, 64], P('pair', 'red'), may hold values from 0 to 1, as said below
Outputs:
- ladder_term: bfloat16 [128, 16, 65536], P(None, 'red', 'pair')
The draws below stay inside these ranges and needn't reach their ends.
Inputs may be any that keep to these rules, and one draw needn't show every extreme that they name: `pattern`: in every tile, exactly 8 of each aligned group of 16 blocks are 1.
All inputs are finite; a program needn't handle non-finite values.
Results may differ from the reference program's by a relative error of at most 0.0013.
Values may be sent and summed in bfloat16 or wider, within the bound.
A program may use at most 64 MiB of HBM per device.

```python
import jax
import jax.numpy as jnp

BW = 64
ROWS_DEV = 16
KBQ = 16
NZQ = 8
TILES = 128
PAIRS = 2048
CD_BLOCKS = 64
CD = 4096
AB = 65536


def draw_pattern(key, part):
    key = jax.random.fold_in(key, 7)
    quarters = CD_BLOCKS // KBQ
    scores = jax.random.randint(key, (TILES, quarters, KBQ), 0, 1 << 20) * KBQ + jnp.arange(KBQ, dtype=jnp.int32)
    block_rank = jnp.argsort(jnp.argsort(scores, axis=-1), axis=-1)
    return (block_rank < NZQ).astype(jnp.int32).reshape(TILES, CD_BLOCKS)


def level_of(rng, dims, shards, smallest, high):
    gain = 1.0
    for dim, parts in shards:
        heights = jax.random.uniform(jax.random.fold_in(jax.random.fold_in(rng, 6), dim), (parts,), jnp.float32, smallest / len(shards), high / len(shards))
        gain = gain * jnp.repeat(jnp.exp(heights), dims[dim] // parts).reshape((-1,) + (1,) * (len(dims) - 1 - dim))
    return gain


def normal_values(own_key, extent, spread, reach, split=(), kind=jnp.bfloat16):
    array = jax.random.normal(own_key, extent, jnp.float32) * spread
    if len(split) > 0:
        array = level_of(own_key, extent, split, -0.22, 0.18) * array
    return jnp.clip(array, min=-reach, max=reach).astype(kind)


def setup_inputs(seed: int = 0) -> dict:
    seeds = jax.random.split(jax.random.key(seed), 4)
    return {
        "amplitudes": normal_values(seeds[0], (PAIRS, CD), 1.0, 6.0, ((0, 128), (1, 4))),
        "integrals": normal_values(seeds[1], (CD, AB), (CD // 2) ** -0.5, 0.125, ((0, 4), (1, 128))),
        "pattern": draw_pattern(jax.random.fold_in(seeds[3], 71), 0),
    }


def reference(amplitudes, integrals, pattern):
    expanded = jnp.repeat(jnp.repeat(pattern, ROWS_DEV, axis=0), BW, axis=1).astype(jnp.bfloat16)
    masked = amplitudes * expanded
    ladder = jnp.dot(masked, integrals, preferred_element_type=jnp.float32)
    return ladder.astype(jnp.bfloat16).reshape(TILES, ROWS_DEV, AB)
```

```python
import functools

import jax
import jax.numpy as jnp
from jax import lax
from jax.experimental import pallas as pl
from jax.experimental.pallas import tpu as pltpu
from jax.sharding import PartitionSpec as P

MESH = pl.DeviceIdType.MESH
NY, NZ, NX = 4, 16, 4
OFFSETS = (0, 1, -1, 2, -2, 3, -3, 4, -4, 5, -5, 6, -6, 7, -7, 8)
SLOT = {off % NZ: slot for slot, off in enumerate(OFFSETS)}
BATCHES = ((0, 1), (1, 5), (5, 9), (9, 13), (13, 16))
ROWS = 16
BW = 64
BLOCKS = 16
KEPT = 8
LEVELS = 32760.0


def both_halves(pair):
    low = lax.broadcasted_iota(jnp.int32, pair.shape, 1) < BW
    turned = pltpu.roll(pair, BW, 1)
    return jnp.where(low, pair, turned), jnp.where(low, turned, pair)


def kernel(
    amp_ref, pat_ref, int_ref, out_ref,
    tiles, dense, sums, b_ref, xs, xr, ss, sr,
    b_sem, zs_sem, zr_sem, ys_sem, yr_sem, cs_sem, cr_sem, xs_sem, xr_sem, ss_sem, sr_sem,
):
    pair, r = lax.axis_index("pair"), lax.axis_index("red")
    y, z, c = pair // (2 * NZ), (pair // 2) % NZ, pair % 2

    def at_y(d):
        return (((y + d) % NY) * (2 * NZ) + z * 2 + c, r)

    def at_z(d):
        return (y * (2 * NZ) + ((z + d) % NZ) * 2 + c, r)

    def at_x(d):
        return (pair, (r + d) % NX)

    sibling = (pair + 1 - 2 * c, r)

    load_b = pltpu.make_async_copy(int_ref, b_ref, b_sem)
    load_b.start()

    barrier = pltpu.get_barrier_semaphore()
    peers = [at_z(d) for d in OFFSETS[1:]] + [at_y(d) for d in range(1, NY)]
    peers += [at_x(d) for d in range(1, NX)] + [sibling]
    for peer in peers:
        pl.semaphore_signal(barrier, inc=1, device_id=peer, device_id_type=MESH)

    half = lax.broadcasted_iota(jnp.int32, (ROWS, 2 * BW), 1) // BW
    row = lax.broadcasted_iota(jnp.int32, (ROWS, 2 * BW), 0)
    place, seen = [], jnp.int32(0)
    for b in range(BLOCKS):
        keep = pat_ref[0, b] > 0
        place.append(jnp.where(keep, seen, 99))
        seen = seen + jnp.where(keep, 1, 0)
    blocks = []
    for j in range(BLOCKS // 2):
        blocks += both_halves(amp_ref[:, 2 * BW * j : 2 * BW * (j + 1)].astype(jnp.float32))
    code = jnp.zeros((ROWS, 2 * BW), jnp.int32)
    for b in range(BLOCKS):
        code = jnp.where((row == b // 2) & (half == b % 2), place[b], code)
    for j in range(KEPT // 2):
        acc = jnp.zeros((ROWS, 2 * BW), jnp.float32)
        for b in range(2 * j, min(BLOCKS, 2 * j + 10)):
            acc = jnp.where(half + 2 * j == place[b], blocks[b], acc)
        tiles[y, c, 0, :, 2 * BW * j : 2 * BW * (j + 1)] = acc.astype(jnp.bfloat16)
    tiles[y, c, 0, :, KEPT * BW :] = code.astype(jnp.float32).astype(jnp.bfloat16)

    pl.semaphore_wait(barrier, len(peers))

    def remote(src, dst, send, recv, device):
        return pltpu.make_async_remote_copy(
            src_ref=src, dst_ref=dst, send_sem=send, recv_sem=recv,
            device_id=device, device_id_type=MESH,
        )

    def z_copy(d):
        slot = SLOT[-d % NZ]
        return remote(
            tiles.at[y, c, 0], tiles.at[y, c, slot], zs_sem.at[slot], zr_sem.at[slot], at_z(d)
        )

    def y_copy(d, k):
        a, b = BATCHES[k]
        part = tiles.at[y, c, a:b]
        return remote(part, part, ys_sem.at[d - 1, k], yr_sem.at[d - 1, k], at_y(d))

    def core_copy(d, k):
        a, b = BATCHES[k]
        part = tiles.at[(y - d + NY) % NY, c, a:b]
        return remote(part, part, cs_sem.at[d, k], cr_sem.at[d, k], sibling)

    def x_copies(d, k):
        a, b = BATCHES[k]
        rows = slice(32 * a, 32 * b)
        return (
            remote(ss.at[d - 1, k], sr.at[d - 1, k], ss_sem.at[d - 1, k], sr_sem.at[d - 1, k], at_x(d)),
            remote(xs.at[d - 1, rows], xr.at[d - 1, rows], xs_sem.at[d - 1, k], xr_sem.at[d - 1, k], at_x(d)),
        )

    def from_z(k):
        a, b = BATCHES[k]
        if k:
            for slot in range(a, b):
                z_copy(-OFFSETS[slot]).wait_recv()
        for d in range(1, NY):
            y_copy(d, k).start()
        core_copy(0, k).start()

    def from_y(k):
        for d in range(1, NY):
            y_copy(d, k).wait_recv()
            core_copy(d, k).start()

    def unpack(k):
        a, b = BATCHES[k]
        n = b - a

        def one(i, _):
            yy, cc, s = i // (2 * n), (i // n) % 2, i % n
            places = tiles[yy, cc, a + s, :, KEPT * BW :].astype(jnp.float32)
            kept = []
            for j in range(KEPT // 2):
                kept += both_halves(
                    tiles[yy, cc, a + s, :, 2 * BW * j : 2 * BW * (j + 1)].astype(jnp.float32)
                )
            for j in range(BLOCKS // 2):
                wanted = jnp.broadcast_to(places[j : j + 1, :], (ROWS, 2 * BW))
                acc = jnp.zeros((ROWS, 2 * BW), jnp.float32)
                for q in range(max(0, 2 * j - 8), min(KEPT, 2 * j + 2)):
                    acc = jnp.where(wanted == float(q), kept[q], acc)
                dense[yy, cc, s, :, 2 * BW * j : 2 * BW * (j + 1)] = acc.astype(jnp.bfloat16)
            return 0

        lax.fori_loop(0, 8 * n, one, 0)

    def multiply(k):
        a, b = BATCHES[k]
        n = b - a

        def one(i, _):
            ys = pl.ds(2 * i, 2)
            lhs = dense[ys, :, 0:n].reshape(4 * n * ROWS, BLOCKS * BW)
            prod = jnp.dot(lhs, b_ref[...], preferred_element_type=jnp.float32)
            prod = prod.reshape(2, 2, n, 2, 8, prod.shape[-1])
            first, second = prod[:, 0], prod[:, 1]
            upper = lax.broadcasted_iota(jnp.int32, first.shape, 3) < 4
            even = jnp.where(upper, first, pltpu.roll(second, 4, 3))
            odd = jnp.where(upper, pltpu.roll(first, 4, 3), second)
            for h in range(2):
                sums[2 * h, ys, a:b] = even[:, :, h]
                sums[2 * h + 1, ys, a:b] = odd[:, :, h]
            return 0

        lax.fori_loop(0, 2, one, 0)

    def compute(k):
        a, b = BATCHES[k]
        n = b - a
        for d in range(NY):
            other = tiles.at[(y - d + NY) % NY, 1 - c, a:b]
            remote(other, other, cs_sem.at[d, k], cr_sem.at[d, k], sibling).wait_recv()
        unpack(k)
        if k == 0:
            load_b.wait()
        multiply(k)
        for d in (2, 1, 3):
            values = sums[(r + d) % NX, :, a:b].reshape(32 * n, sums.shape[-1])
            top = jnp.maximum(jnp.max(jnp.abs(values), axis=0, keepdims=True), 1e-30)
            scaled = jnp.round(values * (LEVELS / top))
            xs[d - 1, 32 * a : 32 * b] = scaled.astype(jnp.int32).astype(jnp.int16)
            ss[d - 1, k] = top * (1.0 / LEVELS)
            for copy in x_copies(d, k):
                copy.start()

    def finish(k):
        a, b = BATCHES[k]
        n = b - a
        total = sums[r, :, a:b].reshape(32 * n, sums.shape[-1])
        for d in (1, 3, 2):
            for copy in x_copies(d, k):
                copy.wait_recv()
            part = xr[d - 1, 32 * a : 32 * b].astype(jnp.int32).astype(jnp.float32)
            total = total + part * sr[d - 1, k]
        total = total.astype(jnp.bfloat16).reshape(NY, n, 8, total.shape[-1])
        for s in range(n):
            out_ref[:, (z + OFFSETS[a + s] + NZ) % NZ] = total[:, s]

    for off in OFFSETS[1:]:
        z_copy(off).start()
    from_z(0)
    from_y(0)
    from_z(1)
    compute(0)
    from_y(1)
    from_z(2)
    compute(1)
    from_y(2)
    from_z(3)
    compute(2)
    finish(0)
    from_y(3)
    from_z(4)
    compute(3)
    finish(1)
    from_y(4)
    compute(4)
    finish(2)
    finish(3)
    finish(4)
    for off in OFFSETS[1:]:
        z_copy(off).wait_send()
    for k in range(len(BATCHES)):
        for d in range(1, NY):
            y_copy(d, k).wait_send()
        for d in range(NY):
            core_copy(d, k).wait_send()
        for d in range(1, NX):
            for copy in x_copies(d, k):
                copy.wait_send()


def shards(amplitudes, integrals, pattern):
    depth, width = integrals.shape
    count = len(BATCHES)
    dma = pltpu.SemaphoreType.DMA
    out = pl.pallas_call(
        kernel,
        out_shape=jax.ShapeDtypeStruct((NY, NZ, 8, width), jnp.bfloat16),
        in_specs=[
            pl.BlockSpec(memory_space=pltpu.VMEM),
            pl.BlockSpec(memory_space=pltpu.SMEM),
            pl.BlockSpec(memory_space=pl.ANY),
        ],
        out_specs=pl.BlockSpec(memory_space=pltpu.VMEM),
        scratch_shapes=[
            pltpu.VMEM((NY, 2, NZ, ROWS, (KEPT + 2) * BW), jnp.bfloat16),
            pltpu.VMEM((NY, 2, 4, ROWS, depth), jnp.bfloat16),
            pltpu.VMEM((NX, NY, NZ, 8, width), jnp.float32),
            pltpu.VMEM((depth, width), jnp.bfloat16),
            pltpu.VMEM((NX - 1, 32 * NZ, width), jnp.int16),
            pltpu.VMEM((NX - 1, 32 * NZ, width), jnp.int16),
            pltpu.VMEM((NX - 1, count, 1, width), jnp.float32),
            pltpu.VMEM((NX - 1, count, 1, width), jnp.float32),
            dma(()),
            dma((NZ,)),
            dma((NZ,)),
            dma((NY - 1, count)),
            dma((NY - 1, count)),
            dma((NY, count)),
            dma((NY, count)),
            dma((NX - 1, count)),
            dma((NX - 1, count)),
            dma((NX - 1, count)),
            dma((NX - 1, count)),
        ],
        compiler_params=pltpu.CompilerParams(
            collective_id=0, has_side_effects=True, vmem_limit_bytes=48 * 2**20
        ),
    )(amplitudes, pattern, integrals)
    return out.reshape(NY * NZ * 2, 4, width)


def solution(mesh):
    placed = (P("pair", "red"), P("red", "pair"), P("pair", "red"))
    return jax.shard_map(
        shards, mesh=mesh, in_specs=placed, out_specs=P(None, "red", "pair"), check_vma=False
    )
```

```python
import jax
import jax.numpy as jnp
from jax import lax
from jax.experimental import pallas as pl
from jax.experimental.pallas import tpu as pltpu
from jax.sharding import PartitionSpec as P

MESH = pl.DeviceIdType.MESH
NY, NZ, NX = 4, 16, 4
OFFSETS = (0, 4, -4, 1, -1, 2, -2, 3, -3, 5, -5, 6, -6, 7, -7, 8)
REACH = 4
SLOT = {off % NZ: slot for slot, off in enumerate(OFFSETS)}
BATCHES = ((0, 1), (1, 5), (5, 9), (9, 13), (13, 16))
ROWS = 16
BW = 64
LANES = 2 * BW
BLOCKS = 16
KEPT = 8
DATA = KEPT * BW
PARTS = 4


def both_halves(pair):
    low = lax.broadcasted_iota(jnp.int32, pair.shape, 1) < BW
    turned = pltpu.roll(pair, BW, 1)
    return jnp.where(low, pair, turned), jnp.where(low, turned, pair)


def turn(arrays):
    upper = lax.broadcasted_iota(jnp.int32, (8, LANES), 0) < 4
    out = []
    for b in range(4):
        part = [v[8 * (b // 2) : 8 * (b // 2) + 8] for v in arrays]
        if b % 2 == 0:
            halves = [jnp.where(upper, part[i], pltpu.roll(part[i + 1], 4, 0)) for i in (0, 2)]
        else:
            halves = [jnp.where(upper, pltpu.roll(part[i], 4, 0), part[i + 1]) for i in (0, 2)]
        out.append(jnp.concatenate(halves, axis=0))
    return out


def kernel(
    amp_ref, pat_ref, int_ref, out_ref,
    pieces, given, tiles, spread, lhs, slices, total,
    b_sem, xs_sem, xr_sem, zs_sem, zr_sem, ys_sem, yr_sem, cs_sem, cr_sem, bs_sem, br_sem,
):
    pair, r = lax.axis_index("pair"), lax.axis_index("red")
    y, z, c = pair // (2 * NZ), (pair // 2) % NZ, pair % 2
    depth, width = int_ref.shape

    def at_y(d):
        return (((y + d) % NY) * (2 * NZ) + z * 2 + c, r)

    def at_z(d):
        return (y * (2 * NZ) + ((z + d) % NZ) * 2 + c, r)

    def at_x(d):
        return (pair, (r + d) % NX)

    sibling = (pair + 1 - 2 * c, r)

    load_b = pltpu.make_async_copy(int_ref, slices.at[r], b_sem)
    load_b.start()

    barrier = pltpu.get_barrier_semaphore()
    near = OFFSETS[1 : 1 + 2 * REACH]
    peers = [at_z(d) for d in near] + [at_y(d) for d in range(1, NY)]
    peers += [at_x(d) for d in range(1, NX)] + [sibling]
    for peer in peers:
        pl.semaphore_signal(barrier, inc=1, device_id=peer, device_id_type=MESH)

    def remote(src, dst, send, recv, device):
        return pltpu.make_async_remote_copy(
            src_ref=src, dst_ref=dst, send_sem=send, recv_sem=recv,
            device_id=device, device_id_type=MESH,
        )

    lane = lax.broadcasted_iota(jnp.int32, (ROWS, LANES), 1)
    row = lax.broadcasted_iota(jnp.int32, (ROWS, LANES), 0)
    place, seen = [], jnp.int32(0)
    for b in range(BLOCKS):
        keep = pat_ref[0, b] > 0
        place.append(jnp.where(keep, seen, 99))
        seen = seen + jnp.where(keep, 1, 0)
    blocks = []
    for j in range(BLOCKS // 2):
        blocks += both_halves(amp_ref[:, LANES * j : LANES * (j + 1)].astype(jnp.float32))
    code = jnp.zeros((ROWS, LANES), jnp.int32)
    for b in range(BLOCKS):
        code = jnp.where(lane == b, place[b], code)
    code = code.astype(jnp.float32).astype(jnp.bfloat16)
    packed = []
    for j in range(KEPT // 2):
        acc = jnp.zeros((ROWS, LANES), jnp.float32)
        for b in range(2 * j, min(BLOCKS, 2 * j + 10)):
            acc = jnp.where(lane // BW + 2 * j == place[b], blocks[b], acc)
        packed.append(acc)
    for d, piece in enumerate(turn(packed)):
        pieces[d, :, :LANES] = piece.astype(jnp.bfloat16)
        pieces[d, :, LANES:] = code
    given[r] = pieces[r]
    wide = lax.broadcasted_iota(jnp.int32, spread.shape, 1) // BW
    spread[...] = jnp.where(
        lax.broadcasted_iota(jnp.int32, spread.shape, 0) == wide, 1.0, 0.0
    ).astype(jnp.bfloat16)

    pl.semaphore_wait(barrier, len(peers))

    def x_copy(d):
        return remote(
            pieces.at[(r + d) % NX], given.at[r], xs_sem.at[d - 1], xr_sem.at[d - 1], at_x(d)
        )

    def z_copy(d):
        slot = SLOT[-d % NZ]
        if abs(d) <= REACH:
            held, device = 0, at_z(d)
        elif abs(d) < 2 * REACH:
            on = REACH if d > 0 else -REACH
            held, device = SLOT[-on % NZ], at_z(d - on)
        else:
            held = jnp.where(c == 0, SLOT[-REACH % NZ], SLOT[REACH])
            device = at_z(REACH - 2 * REACH * c + NZ)
        return remote(
            tiles.at[y, c, held], tiles.at[y, c, slot], zs_sem.at[slot], zr_sem.at[slot], device
        )

    def y_copy(d, k):
        a, b = BATCHES[k]
        part = tiles.at[y, c, a:b]
        return remote(part, part, ys_sem.at[d - 1, k], yr_sem.at[d - 1, k], at_y(d))

    def core_copy(d, k, own=True):
        a, b = BATCHES[k]
        part = tiles.at[(y - d + NY) % NY, c if own else 1 - c, a:b]
        return remote(part, part, cs_sem.at[d, k], cr_sem.at[d, k], sibling)

    rows = depth // PARTS
    half = PARTS // 2

    def own_slice(side, i):
        part = slice(rows * i, rows * (i + 1))
        return remote(
            int_ref.at[part], slices.at[r, part], bs_sem.at[side, i], br_sem.at[side, i], at_x(1 + 2 * side)
        )

    def next_slice(side, i):
        first = rows * (i + half * side)
        part = slices.at[(r + 3 - 2 * side) % NX, first : first + rows]
        return remote(
            part, part, bs_sem.at[side, PARTS + i], br_sem.at[side, PARTS + i], at_x(1 + 2 * side)
        )

    def arrival(side, i):
        if i < PARTS:
            owner, first = (r + 3 - 2 * side) % NX, rows * i
        else:
            owner, first = (r + 2) % NX, rows * (i - PARTS + half * side)
        part = slices.at[owner, first : first + rows]
        return remote(part, part, bs_sem.at[side, i], br_sem.at[side, i], at_x(1 + 2 * side))

    def from_z(k):
        a, b = BATCHES[k]
        if k:
            for slot in range(a, b):
                z_copy(-OFFSETS[slot]).wait_recv()
                if abs(OFFSETS[slot]) == REACH:
                    for more in range(3, 0, -1):
                        z_copy(-OFFSETS[slot] // REACH * (REACH + more)).start()
            if k == 1:
                z_copy(2 * REACH).start()
        for d in range(1, NY):
            y_copy(d, k).start()
        core_copy(0, k).start()

    def from_y(k):
        for d in range(1, NY):
            y_copy(d, k).wait_recv()
            core_copy(d, k).start()

    def send_on(i):
        for side in range(2):
            arrival(side, i + half * side).wait_recv()
            next_slice(side, i).start()

    def unpack(k):
        a, b = BATCHES[k]
        for d in range(NY):
            core_copy(d, k, own=False).wait_recv()

        def one(i, _):
            slot, first = a + i // 2, 2 * (i % 2)
            four = [(first + t // 2, t % 2) for t in range(4)]
            places = jnp.concatenate([tiles[yy, cc, slot, :, DATA:] for yy, cc in four], axis=0)
            wanted = jnp.dot(places, spread[...], preferred_element_type=jnp.float32)
            kept = []
            for yy, cc in four:
                have = []
                for j in range(KEPT // 2):
                    have += both_halves(
                        tiles[yy, cc, slot, :, LANES * j : LANES * (j + 1)].astype(jnp.float32)
                    )
                kept.append(have)
            for j in range(BLOCKS // 2):
                full = []
                for t in range(4):
                    want = wanted[ROWS * t : ROWS * (t + 1), LANES * j : LANES * (j + 1)]
                    acc = jnp.zeros((ROWS, LANES), jnp.float32)
                    for q in range(max(0, 2 * j - 8), min(KEPT, 2 * j + 2)):
                        acc = jnp.where(want == float(q), kept[t][q], acc)
                    full.append(acc)
                for s, piece in enumerate(turn(full)):
                    lhs[s, 2 * a + i, :, LANES * j : LANES * (j + 1)] = piece.astype(jnp.bfloat16)
            return 0

        lax.fori_loop(0, 2 * (b - a), one, 0)

    def multiply(a, b, distances, add):
        def one(i, _):
            columns = pl.ds(pl.multiple_of(i * (width // 2), width // 2), width // 2)
            value = total[32 * a : 32 * b, columns] if add else None
            for d in distances:
                s = (r + d) % NX
                left = lhs[s, 2 * a : 2 * b].reshape(32 * (b - a), depth)
                term = jnp.dot(left, slices[s, :, columns], preferred_element_type=jnp.float32)
                value = term if value is None else value + term
            total[32 * a : 32 * b, columns] = value
            return 0

        lax.fori_loop(0, 2, one, 0)

    for d in (2, 1, 3):
        x_copy(d).start()
    for i in range(PARTS):
        own_slice(0, i).start()
        own_slice(1, (i + half) % PARTS).start()
    for d in range(1, NX):
        came = given.at[(r - d + NX) % NX]
        remote(came, came, xs_sem.at[d - 1], xr_sem.at[d - 1], at_x(d)).wait_recv()
    whole = turn([given[s, :, :LANES].astype(jnp.float32) for s in range(NX)])
    for j in range(KEPT // 2):
        tiles[y, c, 0, :, LANES * j : LANES * (j + 1)] = whole[j].astype(jnp.bfloat16)
    code = jnp.zeros((ROWS, LANES), jnp.float32)
    for s in range(NX):
        code = jnp.where(row // 4 == s, given[s, :, LANES:].astype(jnp.float32), code)
    tiles[y, c, 0, :, DATA:] = code.astype(jnp.bfloat16)

    for off in near:
        z_copy(off).start()
    from_z(0)
    from_z(1)
    from_z(2)
    from_z(3)
    from_z(4)
    send_on(0)
    from_y(0)
    from_y(1)
    unpack(0)
    from_y(2)
    unpack(1)
    from_y(3)
    send_on(1)
    from_y(4)
    unpack(2)
    unpack(3)
    load_b.wait()
    for i in range(PARTS):
        for side in range(2):
            if i // half != side:
                arrival(side, i).wait_recv()
    most = BATCHES[3][1]
    multiply(0, most, (0, 1, 3), False)
    unpack(4)
    multiply(most, NZ, (0, 1, 3), False)
    for i in range(half):
        for side in range(2):
            arrival(side, PARTS + i).wait_recv()
    multiply(0, NZ, (2,), True)
    for slot, off in enumerate(OFFSETS):
        result = total[32 * slot : 32 * (slot + 1)].astype(jnp.bfloat16)
        out_ref[:, (z + off + NZ) % NZ] = result.reshape(NY, 8, width)

    for d in range(1, NX):
        x_copy(d).wait_send()
    for off in OFFSETS[1:]:
        z_copy(off).wait_send()
    for k in range(len(BATCHES)):
        for d in range(1, NY):
            y_copy(d, k).wait_send()
        for d in range(NY):
            core_copy(d, k).wait_send()
    for side in range(2):
        for i in range(PARTS):
            own_slice(side, i).wait_send()
        for i in range(half):
            next_slice(side, i).wait_send()


def shards(amplitudes, integrals, pattern):
    depth, width = integrals.shape
    count = len(BATCHES)
    dma = pltpu.SemaphoreType.DMA
    out = pl.pallas_call(
        kernel,
        out_shape=jax.ShapeDtypeStruct((NY, NZ, 8, width), jnp.bfloat16),
        in_specs=[
            pl.BlockSpec(memory_space=pltpu.VMEM),
            pl.BlockSpec(memory_space=pltpu.SMEM),
            pl.BlockSpec(memory_space=pltpu.HBM),
        ],
        out_specs=pl.BlockSpec(memory_space=pltpu.VMEM),
        scratch_shapes=[
            pltpu.VMEM((NX, ROWS, 2 * LANES), jnp.bfloat16),
            pltpu.VMEM((NX, ROWS, 2 * LANES), jnp.bfloat16),
            pltpu.VMEM((NY, 2, NZ, ROWS, DATA + LANES), jnp.bfloat16),
            pltpu.VMEM((LANES, depth), jnp.bfloat16),
            pltpu.VMEM((NX, 2 * NZ, ROWS, depth), jnp.bfloat16),
            pltpu.VMEM((NX, depth, width), jnp.bfloat16),
            pltpu.VMEM((32 * NZ, width), jnp.float32),
            dma(()),
            dma((NX - 1,)),
            dma((NX - 1,)),
            dma((NZ,)),
            dma((NZ,)),
            dma((NY - 1, count)),
            dma((NY - 1, count)),
            dma((NY, count)),
            dma((NY, count)),
            dma((2, PARTS + PARTS // 2)),
            dma((2, PARTS + PARTS // 2)),
        ],
        compiler_params=pltpu.CompilerParams(
            collective_id=0, has_side_effects=True, vmem_limit_bytes=62 * 2**20
        ),
    )(amplitudes, pattern, integrals)
    return out.reshape(NY * NZ * 2, 4, width)


def solution(mesh):
    placed = (P("pair", "red"), P("red", "pair"), P("pair", "red"))
    return jax.shard_map(
        shards, mesh=mesh, in_specs=placed, out_specs=P(None, "red", "pair"), check_vma=False
    )
```

```python
import jax
import jax.numpy as jnp
from jax import lax
from jax.experimental import pallas as pl
from jax.experimental.pallas import tpu as pltpu
from jax.sharding import PartitionSpec as P

MESH = pl.DeviceIdType.MESH
NY, NZ, NX = 4, 16, 4
OFFSETS = (0, 4, -4, 1, -1, 2, -2, 3, -3, 5, -5, 6, -6, 7, -7, 8)
REACH = 4
SLOT = {off % NZ: slot for slot, off in enumerate(OFFSETS)}
BATCHES = ((0, 1), (1, 5), (5, 9), (9, 13), (13, 16))
ROWS = 16
BW = 64
LANES = 2 * BW
BLOCKS = 16
KEPT = 8
DATA = KEPT * BW
PARTS = 4


def both_halves(pair):
    low = lax.broadcasted_iota(jnp.int32, pair.shape, 1) < BW
    turned = pltpu.roll(pair, BW, 1)
    return jnp.where(low, pair, turned), jnp.where(low, turned, pair)


def turn(arrays):
    upper = lax.broadcasted_iota(jnp.int32, (8, LANES), 0) < 4
    out = []
    for b in range(4):
        part = [v[8 * (b // 2) : 8 * (b // 2) + 8] for v in arrays]
        if b % 2 == 0:
            halves = [jnp.where(upper, part[i], pltpu.roll(part[i + 1], 4, 0)) for i in (0, 2)]
        else:
            halves = [jnp.where(upper, pltpu.roll(part[i], 4, 0), part[i + 1]) for i in (0, 2)]
        out.append(jnp.concatenate(halves, axis=0))
    return out


def kernel(
    amp_ref, pat_ref, int_ref, out_ref,
    pieces, given, tiles, spread, lhs, slices, total,
    b_sem, xs_sem, xr_sem, zs_sem, zr_sem, ys_sem, yr_sem, cs_sem, cr_sem, bs_sem, br_sem, hello,
):
    pair, r = lax.axis_index("pair"), lax.axis_index("red")
    y, z, c = pair // (2 * NZ), (pair // 2) % NZ, pair % 2
    depth, width = int_ref.shape

    def at_y(d):
        return (((y + d) % NY) * (2 * NZ) + z * 2 + c, r)

    def at_z(d):
        return (y * (2 * NZ) + ((z + d) % NZ) * 2 + c, r)

    def at_x(d):
        return (pair, (r + d) % NX)

    sibling = (pair + 1 - 2 * c, r)

    load_b = pltpu.make_async_copy(int_ref, slices.at[r], b_sem)
    load_b.start()

    barrier = pltpu.get_barrier_semaphore()
    near = OFFSETS[1 : 1 + 2 * REACH]
    peers = [at_z(-d) for d in range(1, REACH + 1)] + [at_y(d) for d in range(1, NY)]
    peers += [at_x(d) for d in range(1, NX)] + [sibling]
    for peer in peers:
        pl.semaphore_signal(barrier, inc=1, device_id=peer, device_id_type=MESH)

    def remote(src, dst, send, recv, device):
        return pltpu.make_async_remote_copy(
            src_ref=src, dst_ref=dst, send_sem=send, recv_sem=recv,
            device_id=device, device_id_type=MESH,
        )

    lane = lax.broadcasted_iota(jnp.int32, (ROWS, LANES), 1)
    row = lax.broadcasted_iota(jnp.int32, (ROWS, LANES), 0)
    place, seen = [], jnp.int32(0)
    for b in range(BLOCKS):
        keep = pat_ref[0, b] > 0
        place.append(jnp.where(keep, seen, 99))
        seen = seen + jnp.where(keep, 1, 0)
    blocks = []
    for j in range(BLOCKS // 2):
        blocks += both_halves(amp_ref[:, LANES * j : LANES * (j + 1)].astype(jnp.float32))
    code = jnp.zeros((ROWS, LANES), jnp.int32)
    for b in range(BLOCKS):
        code = jnp.where(lane == b, place[b], code)
    code = code.astype(jnp.float32).astype(jnp.bfloat16)
    packed = []
    for j in range(KEPT // 2):
        acc = jnp.zeros((ROWS, LANES), jnp.float32)
        for b in range(2 * j, min(BLOCKS, 2 * j + 10)):
            acc = jnp.where(lane // BW + 2 * j == place[b], blocks[b], acc)
        packed.append(acc)
    for d, piece in enumerate(turn(packed)):
        pieces[d, :, :LANES] = piece.astype(jnp.bfloat16)
        pieces[d, :, LANES:] = code
    given[r] = pieces[r]
    wide = lax.broadcasted_iota(jnp.int32, spread.shape, 1) // BW
    spread[...] = jnp.where(
        lax.broadcasted_iota(jnp.int32, spread.shape, 0) == wide, 1.0, 0.0
    ).astype(jnp.bfloat16)

    pl.semaphore_wait(barrier, len(peers))

    def x_copy(d):
        return remote(
            pieces.at[(r + d) % NX], given.at[r], xs_sem.at[d - 1], xr_sem.at[d - 1], at_x(d)
        )

    def z_copy(d):
        slot = SLOT[-d % NZ]
        if abs(d) <= REACH:
            held, device = 0, at_z(d)
        elif abs(d) < 2 * REACH:
            on = REACH if d > 0 else -REACH
            held, device = SLOT[-on % NZ], at_z(d - on)
        else:
            held = jnp.where(c == 0, SLOT[-REACH % NZ], SLOT[REACH])
            device = at_z(REACH - 2 * REACH * c + NZ)
        return remote(
            tiles.at[y, c, held], tiles.at[y, c, slot], zs_sem.at[slot], zr_sem.at[slot], device
        )

    def y_copy(d, k):
        a, b = BATCHES[k]
        part = tiles.at[y, c, a:b]
        return remote(part, part, ys_sem.at[d - 1, k], yr_sem.at[d - 1, k], at_y(d))

    def core_copy(d, k, own=True):
        a, b = BATCHES[k]
        part = tiles.at[(y - d + NY) % NY, c if own else 1 - c, a:b]
        return remote(part, part, cs_sem.at[d, k], cr_sem.at[d, k], sibling)

    rows = depth // PARTS
    half = PARTS // 2

    def own_slice(side, i):
        part = slice(rows * i, rows * (i + 1))
        return remote(
            int_ref.at[part], slices.at[r, part], bs_sem.at[side, i], br_sem.at[side, i], at_x(1 + 2 * side)
        )

    def next_slice(side, i):
        first = rows * (i + half * side)
        part = slices.at[(r + 3 - 2 * side) % NX, first : first + rows]
        return remote(
            part, part, bs_sem.at[side, PARTS + i], br_sem.at[side, PARTS + i], at_x(1 + 2 * side)
        )

    def arrival(side, i):
        if i < PARTS:
            owner, first = (r + 3 - 2 * side) % NX, rows * i
        else:
            owner, first = (r + 2) % NX, rows * (i - PARTS + half * side)
        part = slices.at[owner, first : first + rows]
        return remote(part, part, bs_sem.at[side, i], br_sem.at[side, i], at_x(1 + 2 * side))

    def from_z(k):
        a, b = BATCHES[k]
        if k:
            for slot in range(a, b):
                z_copy(-OFFSETS[slot]).wait_recv()
                if abs(OFFSETS[slot]) == REACH:
                    for more in range(3, 0, -1):
                        z_copy(-OFFSETS[slot] // REACH * (REACH + more)).start()
            if k == 1:
                z_copy(2 * REACH).start()
        for d in range(1, NY):
            y_copy(d, k).start()
        core_copy(0, k).start()

    def from_y(k):
        for d in range(1, NY):
            y_copy(d, k).wait_recv()
            core_copy(d, k).start()

    def send_on(i):
        for side in range(2):
            arrival(side, i + half * side).wait_recv()
            next_slice(side, i).start()

    def unpack(k):
        a, b = BATCHES[k]
        for d in range(NY):
            core_copy(d, k, own=False).wait_recv()

        def one(i, _):
            slot, first = a + i // 2, 2 * (i % 2)
            four = [(first + t // 2, t % 2) for t in range(4)]
            places = jnp.concatenate([tiles[yy, cc, slot, :, DATA:] for yy, cc in four], axis=0)
            wanted = jnp.dot(places, spread[...], preferred_element_type=jnp.float32)
            kept = []
            for yy, cc in four:
                have = []
                for j in range(KEPT // 2):
                    have += both_halves(
                        tiles[yy, cc, slot, :, LANES * j : LANES * (j + 1)].astype(jnp.float32)
                    )
                kept.append(have)
            for j in range(BLOCKS // 2):
                full = []
                for t in range(4):
                    want = wanted[ROWS * t : ROWS * (t + 1), LANES * j : LANES * (j + 1)]
                    acc = jnp.zeros((ROWS, LANES), jnp.float32)
                    for q in range(max(0, 2 * j - 8), min(KEPT, 2 * j + 2)):
                        acc = jnp.where(want == float(q), kept[t][q], acc)
                    full.append(acc)
                for s, piece in enumerate(turn(full)):
                    lhs[s, 2 * a + i, :, LANES * j : LANES * (j + 1)] = piece.astype(jnp.bfloat16)
            return 0

        lax.fori_loop(0, 2 * (b - a), one, 0)

    def multiply(a, b, distances, add):
        def one(i, _):
            columns = pl.ds(pl.multiple_of(i * (width // 2), width // 2), width // 2)
            value = total[32 * a : 32 * b, columns] if add else None
            for d in distances:
                s = (r + d) % NX
                left = lhs[s, 2 * a : 2 * b].reshape(32 * (b - a), depth)
                term = jnp.dot(left, slices[s, :, columns], preferred_element_type=jnp.float32)
                value = term if value is None else value + term
            total[32 * a : 32 * b, columns] = value
            return 0

        lax.fori_loop(0, 2, one, 0)

    for d in range(1, REACH + 1):
        pl.semaphore_signal(hello.at[d - 1], inc=1, device_id=at_z(d), device_id_type=MESH)
    for d in (2, 1, 3):
        x_copy(d).start()
    for i in range(PARTS):
        own_slice(0, i).start()
        own_slice(1, (i + half) % PARTS).start()
    for d in range(1, NX):
        came = given.at[(r - d + NX) % NX]
        remote(came, came, xs_sem.at[d - 1], xr_sem.at[d - 1], at_x(d)).wait_recv()
    whole = turn([given[s, :, :LANES].astype(jnp.float32) for s in range(NX)])
    for j in range(KEPT // 2):
        tiles[y, c, 0, :, LANES * j : LANES * (j + 1)] = whole[j].astype(jnp.bfloat16)
    code = jnp.zeros((ROWS, LANES), jnp.float32)
    for s in range(NX):
        code = jnp.where(row // 4 == s, given[s, :, LANES:].astype(jnp.float32), code)
    tiles[y, c, 0, :, DATA:] = code.astype(jnp.bfloat16)

    for off in near:
        if off > 0:
            z_copy(off).start()
    from_z(0)
    from_y(0)
    for d in (4, 1, 2, 3):
        pl.semaphore_wait(hello.at[d - 1], 1)
        z_copy(-d).start()
    from_z(1)
    from_z(2)
    from_z(3)
    from_z(4)
    send_on(0)
    from_y(1)
    unpack(0)
    from_y(2)
    unpack(1)
    from_y(3)
    send_on(1)
    from_y(4)
    unpack(2)
    unpack(3)
    load_b.wait()
    for i in range(PARTS):
        for side in range(2):
            if i // half != side:
                arrival(side, i).wait_recv()
    most = BATCHES[-2][1]
    multiply(0, most, (0, 1, 3), False)
    unpack(4)
    multiply(most, NZ, (0, 1, 3), False)
    for i in range(half):
        for side in range(2):
            arrival(side, PARTS + i).wait_recv()
    multiply(0, NZ, (2,), True)
    for slot, off in enumerate(OFFSETS):
        result = total[32 * slot : 32 * (slot + 1)].astype(jnp.bfloat16)
        place_in = 2 * ((z + off + NZ) % NZ)
        for yy in range(NY):
            for cc in range(2):
                first = 8 * yy + 4 * cc
                out_ref[2 * NZ * yy + cc + place_in] = result[first : first + 4]

    for d in range(1, NX):
        x_copy(d).wait_send()
    for off in OFFSETS[1:]:
        z_copy(off).wait_send()
    for k in range(len(BATCHES)):
        for d in range(1, NY):
            y_copy(d, k).wait_send()
        for d in range(NY):
            core_copy(d, k).wait_send()
    for side in range(2):
        for i in range(PARTS):
            own_slice(side, i).wait_send()
        for i in range(half):
            next_slice(side, i).wait_send()


def shards(amplitudes, integrals, pattern):
    depth, width = integrals.shape
    count = len(BATCHES)
    dma = pltpu.SemaphoreType.DMA
    out = pl.pallas_call(
        kernel,
        out_shape=jax.ShapeDtypeStruct((2 * NY * NZ, 4, width), jnp.bfloat16),
        in_specs=[
            pl.BlockSpec(memory_space=pltpu.VMEM),
            pl.BlockSpec(memory_space=pltpu.SMEM),
            pl.BlockSpec(memory_space=pltpu.HBM),
        ],
        out_specs=pl.BlockSpec(memory_space=pltpu.VMEM),
        scratch_shapes=[
            pltpu.VMEM((NX, ROWS, 2 * LANES), jnp.bfloat16),
            pltpu.VMEM((NX, ROWS, 2 * LANES), jnp.bfloat16),
            pltpu.VMEM((NY, 2, NZ, ROWS, DATA + LANES), jnp.bfloat16),
            pltpu.VMEM((LANES, depth), jnp.bfloat16),
            pltpu.VMEM((NX, 2 * NZ, ROWS, depth), jnp.bfloat16),
            pltpu.VMEM((NX, depth, width), jnp.bfloat16),
            pltpu.VMEM((32 * NZ, width), jnp.float32),
            dma(()),
            dma((NX - 1,)),
            dma((NX - 1,)),
            dma((NZ,)),
            dma((NZ,)),
            dma((NY - 1, count)),
            dma((NY - 1, count)),
            dma((NY, count)),
            dma((NY, count)),
            dma((2, PARTS + PARTS // 2)),
            dma((2, PARTS + PARTS // 2)),
            pltpu.SemaphoreType.REGULAR((REACH,)),
        ],
        compiler_params=pltpu.CompilerParams(
            collective_id=0, has_side_effects=True, vmem_limit_bytes=62 * 2**20
        ),
    )(amplitudes, pattern, integrals)
    return out


def solution(mesh):
    placed = (P("pair", "red"), P("red", "pair"), P("pair", "red"))
    return jax.shard_map(
        shards, mesh=mesh, in_specs=placed, out_specs=P(None, "red", "pair"), check_vma=False
    )
```

```python
import jax
import jax.numpy as jnp
from jax import lax
from jax.experimental import pallas as pl
from jax.experimental.pallas import tpu as pltpu
from jax.sharding import PartitionSpec as P

MESH = pl.DeviceIdType.MESH
NY, NZ, NX = 4, 16, 4
OFFSETS = (0, 1, -1, 2, -2, 4, -4, 3, -3, 5, -5, 6, -6, 7, -7, 8)
REACH = 4
SLOT = {off % NZ: slot for slot, off in enumerate(OFFSETS)}
PLANE = 1
BATCHES = ((0, 1), (1, 5), (5, 9), (9, 13), (13, 16))
ROWS = 16
BW = 64
LANES = 2 * BW
BLOCKS = 16
KEPT = 8
DATA = KEPT * BW
PARTS = 4


def both_halves(pair):
    low = lax.broadcasted_iota(jnp.int32, pair.shape, 1) < BW
    turned = pltpu.roll(pair, BW, 1)
    return jnp.where(low, pair, turned), jnp.where(low, turned, pair)


def turn(arrays):
    upper = lax.broadcasted_iota(jnp.int32, (8, LANES), 0) < 4
    out = []
    for b in range(4):
        part = [v[8 * (b // 2) : 8 * (b // 2) + 8] for v in arrays]
        if b % 2 == 0:
            halves = [jnp.where(upper, part[i], pltpu.roll(part[i + 1], 4, 0)) for i in (0, 2)]
        else:
            halves = [jnp.where(upper, pltpu.roll(part[i], 4, 0), part[i + 1]) for i in (0, 2)]
        out.append(jnp.concatenate(halves, axis=0))
    return out


def kernel(
    amp_ref, pat_ref, int_ref, out_ref,
    pieces, given, tiles, spread, lhs, slices, total,
    b_sem, xs_sem, xr_sem, zs_sem, zr_sem, ys_sem, yr_sem, cs_sem, cr_sem, bs_sem, br_sem, hello,
):
    pair, r = lax.axis_index("pair"), lax.axis_index("red")
    y, z, c = pair // (2 * NZ), (pair // 2) % NZ, pair % 2
    depth, width = int_ref.shape

    def at_y(d):
        return (((y + d) % NY) * (2 * NZ) + z * 2 + c, r)

    def at_z(d):
        return (y * (2 * NZ) + ((z + d) % NZ) * 2 + c, r)

    def at_x(d):
        return (pair, (r + d) % NX)

    sibling = (pair + 1 - 2 * c, r)

    load_b = pltpu.make_async_copy(int_ref, slices.at[r], b_sem)
    load_b.start()

    barrier = pltpu.get_barrier_semaphore()
    peers = [at_z(-1), at_z(-2)] + [at_y(d) for d in range(1, NY)]
    peers += [at_x(d) for d in range(1, NX)] + [sibling]
    for peer in peers:
        pl.semaphore_signal(barrier, inc=1, device_id=peer, device_id_type=MESH)

    def remote(src, dst, send, recv, device):
        return pltpu.make_async_remote_copy(
            src_ref=src, dst_ref=dst, send_sem=send, recv_sem=recv,
            device_id=device, device_id_type=MESH,
        )

    lane = lax.broadcasted_iota(jnp.int32, (ROWS, LANES), 1)
    row = lax.broadcasted_iota(jnp.int32, (ROWS, LANES), 0)
    place, seen = [], jnp.int32(0)
    for b in range(BLOCKS):
        keep = pat_ref[0, b] > 0
        place.append(jnp.where(keep, seen, 99))
        seen = seen + jnp.where(keep, 1, 0)
    blocks = []
    for j in range(BLOCKS // 2):
        blocks += both_halves(amp_ref[:, LANES * j : LANES * (j + 1)].astype(jnp.float32))
    code = jnp.zeros((ROWS, LANES), jnp.int32)
    for b in range(BLOCKS):
        code = jnp.where(lane == b, place[b], code)
    code = code.astype(jnp.float32).astype(jnp.bfloat16)
    packed = []
    for j in range(KEPT // 2):
        acc = jnp.zeros((ROWS, LANES), jnp.float32)
        for b in range(2 * j, min(BLOCKS, 2 * j + 10)):
            acc = jnp.where(lane // BW + 2 * j == place[b], blocks[b], acc)
        packed.append(acc)
    for d, piece in enumerate(turn(packed)):
        pieces[d, :, :LANES] = piece.astype(jnp.bfloat16)
        pieces[d, :, LANES:] = code
    given[r] = pieces[r]
    wide = lax.broadcasted_iota(jnp.int32, spread.shape, 1) // BW
    spread[...] = jnp.where(
        lax.broadcasted_iota(jnp.int32, spread.shape, 0) == wide, 1.0, 0.0
    ).astype(jnp.bfloat16)

    pl.semaphore_wait(barrier, len(peers))

    def x_copy(d):
        return remote(
            pieces.at[(r + d) % NX], given.at[r], xs_sem.at[d - 1], xr_sem.at[d - 1], at_x(d)
        )

    def z_copy(d):
        slot = SLOT[-d % NZ]
        if abs(d) <= REACH:
            held, device = 0, at_z(d)
        elif abs(d) < 2 * REACH:
            on = REACH if d > 0 else -REACH
            held, device = SLOT[-on % NZ], at_z(d - on)
        else:
            held = jnp.where(c == 0, SLOT[-REACH % NZ], SLOT[REACH])
            device = at_z(REACH - 2 * REACH * c + NZ)
        return remote(
            tiles.at[y, c, held], tiles.at[y, c, slot], zs_sem.at[slot], zr_sem.at[slot], device
        )

    def plane_copy(d):
        slot = SLOT[-d % NZ]
        return remote(
            tiles.at[:, c, 0], tiles.at[:, c, slot], zs_sem.at[slot], zr_sem.at[slot], at_z(d)
        )

    def plane_core_copy(own=True):
        a, b = BATCHES[PLANE]
        part = tiles.at[:, c if own else 1 - c, a:b]
        return remote(part, part, cs_sem.at[0, PLANE], cr_sem.at[0, PLANE], sibling)

    def y_copy(d, k):
        a, b = BATCHES[k]
        part = tiles.at[y, c, a:b]
        return remote(part, part, ys_sem.at[d - 1, k], yr_sem.at[d - 1, k], at_y(d))

    def core_copy(d, k, own=True):
        a, b = BATCHES[k]
        part = tiles.at[(y - d + NY) % NY, c if own else 1 - c, a:b]
        return remote(part, part, cs_sem.at[d, k], cr_sem.at[d, k], sibling)

    rows = depth // PARTS
    half = PARTS // 2

    def own_slice(side, i):
        part = slice(rows * i, rows * (i + 1))
        return remote(
            int_ref.at[part], slices.at[r, part], bs_sem.at[side, i], br_sem.at[side, i], at_x(1 + 2 * side)
        )

    def next_slice(side, i):
        first = rows * (i + half * side)
        part = slices.at[(r + 3 - 2 * side) % NX, first : first + rows]
        return remote(
            part, part, bs_sem.at[side, PARTS + i], br_sem.at[side, PARTS + i], at_x(1 + 2 * side)
        )

    def arrival(side, i):
        if i < PARTS:
            owner, first = (r + 3 - 2 * side) % NX, rows * i
        else:
            owner, first = (r + 2) % NX, rows * (i - PARTS + half * side)
        part = slices.at[owner, first : first + rows]
        return remote(part, part, bs_sem.at[side, i], br_sem.at[side, i], at_x(1 + 2 * side))

    def from_z(k):
        a, b = BATCHES[k]
        if k:
            for slot in range(a, b):
                z_copy(-OFFSETS[slot]).wait_recv()
                if abs(OFFSETS[slot]) == REACH:
                    for more in range(3, 0, -1):
                        z_copy(-OFFSETS[slot] // REACH * (REACH + more)).start()
            if k == 2:
                z_copy(2 * REACH).start()
        for d in (2, 1, 3):
            y_copy(d, k).start()
        core_copy(0, k).start()

    def from_y(k):
        for d in (1, 3, 2):
            y_copy(d, k).wait_recv()
            core_copy(d, k).start()

    def send_on(i):
        for side in range(2):
            arrival(side, i + half * side).wait_recv()
            next_slice(side, i).start()

    def unpack(k):
        a, b = BATCHES[k]
        if k == PLANE:
            plane_core_copy(own=False).wait_recv()
        else:
            for d in range(NY):
                core_copy(d, k, own=False).wait_recv()

        def one(i, _):
            slot, first = a + i // 2, 2 * (i % 2)
            four = [(first + t // 2, t % 2) for t in range(4)]
            places = jnp.concatenate([tiles[yy, cc, slot, :, DATA:] for yy, cc in four], axis=0)
            wanted = jnp.dot(places, spread[...], preferred_element_type=jnp.float32)
            wanted = wanted.astype(jnp.bfloat16)
            kept = []
            for yy, cc in four:
                have = []
                for j in range(KEPT // 2):
                    have += both_halves(
                        tiles[yy, cc, slot, :, LANES * j : LANES * (j + 1)].astype(jnp.float32)
                    )
                kept.append([block.astype(jnp.bfloat16) for block in have])
            for j in range(BLOCKS // 2):
                full = []
                for t in range(4):
                    want = wanted[ROWS * t : ROWS * (t + 1), LANES * j : LANES * (j + 1)]
                    acc = jnp.zeros((ROWS, LANES), jnp.bfloat16)
                    for q in range(max(0, 2 * j - 8), min(KEPT, 2 * j + 2)):
                        acc = jnp.where(want == jnp.bfloat16(q), kept[t][q], acc)
                    full.append(acc.astype(jnp.float32))
                for s, piece in enumerate(turn(full)):
                    lhs[s, 2 * a + i, :, LANES * j : LANES * (j + 1)] = piece.astype(jnp.bfloat16)
            return 0

        lax.fori_loop(0, 2 * (b - a), one, 0)

    def multiply(a, b, distances, add):
        def one(i, _):
            columns = pl.ds(pl.multiple_of(i * (width // 2), width // 2), width // 2)
            value = total[32 * a : 32 * b, columns] if add else None
            for d in distances:
                s = (r + d) % NX
                left = lhs[s, 2 * a : 2 * b].reshape(32 * (b - a), depth)
                term = jnp.dot(left, slices[s, :, columns], preferred_element_type=jnp.float32)
                value = term if value is None else value + term
            total[32 * a : 32 * b, columns] = value
            return 0

        lax.fori_loop(0, 2, one, 0)

    for d in (1, 2):
        pl.semaphore_signal(hello.at[d - 1], inc=1, device_id=at_z(d), device_id_type=MESH)
    for d in (2, 1, 3):
        x_copy(d).start()
    for i in range(PARTS):
        own_slice(0, i).start()
        own_slice(1, (i + half) % PARTS).start()
    for d in range(1, NX):
        came = given.at[(r - d + NX) % NX]
        remote(came, came, xs_sem.at[d - 1], xr_sem.at[d - 1], at_x(d)).wait_recv()
    whole = turn([given[s, :, :LANES].astype(jnp.float32) for s in range(NX)])
    for j in range(KEPT // 2):
        tiles[y, c, 0, :, LANES * j : LANES * (j + 1)] = whole[j].astype(jnp.bfloat16)
    code = jnp.zeros((ROWS, LANES), jnp.float32)
    for s in range(NX):
        code = jnp.where(row // 4 == s, given[s, :, LANES:].astype(jnp.float32), code)
    tiles[y, c, 0, :, DATA:] = code.astype(jnp.bfloat16)

    from_z(0)
    pl.semaphore_wait(hello.at[1], 1)
    pl.semaphore_wait(hello.at[0], 1)
    pl.semaphore_signal(hello.at[2], inc=1, device_id=at_z(-2), device_id_type=MESH)
    pl.semaphore_signal(hello.at[3], inc=1, device_id=at_z(2), device_id_type=MESH)
    pl.semaphore_wait(hello.at[2], 1)
    z_copy(4).start()
    pl.semaphore_wait(hello.at[3], 1)
    for d in (-4, 3, -3):
        z_copy(d).start()
    from_y(0)
    for d in (1, -1, 2, -2):
        plane_copy(d).start()
    from_z(2)
    for d in (1, -1, 2, -2):
        plane_copy(-d).wait_recv()
    plane_core_copy().start()
    from_z(3)
    from_z(4)
    send_on(0)
    from_y(2)
    unpack(0)
    unpack(1)
    from_y(3)
    send_on(1)
    unpack(2)
    load_b.wait()
    for i in range(PARTS):
        for side in range(2):
            if i // half != side:
                arrival(side, i).wait_recv()
    multiply(0, BATCHES[2][1], (0, 1, 3), False)
    from_y(4)
    unpack(3)
    middle, most = BATCHES[2][1], BATCHES[-2][1]
    multiply(middle, most, (0, 1, 3), False)
    unpack(4)
    multiply(most, NZ, (0, 1, 3), False)
    for i in range(half):
        for side in range(2):
            arrival(side, PARTS + i).wait_recv()
    multiply(0, NZ, (2,), True)
    for slot, off in enumerate(OFFSETS):
        result = total[32 * slot : 32 * (slot + 1)].astype(jnp.bfloat16)
        place_in = 2 * ((z + off + NZ) % NZ)
        for yy in range(NY):
            for cc in range(2):
                first = 8 * yy + 4 * cc
                out_ref[2 * NZ * yy + cc + place_in] = result[first : first + 4]

    for d in range(1, NX):
        x_copy(d).wait_send()
    for off in OFFSETS[1:]:
        if abs(off) <= 2:
            plane_copy(off).wait_send()
        else:
            z_copy(off).wait_send()
    plane_core_copy().wait_send()
    for k in range(len(BATCHES)):
        if k == PLANE:
            continue
        for d in range(1, NY):
            y_copy(d, k).wait_send()
        for d in range(NY):
            core_copy(d, k).wait_send()
    for side in range(2):
        for i in range(PARTS):
            own_slice(side, i).wait_send()
        for i in range(half):
            next_slice(side, i).wait_send()


def shards(amplitudes, integrals, pattern):
    depth, width = integrals.shape
    count = len(BATCHES)
    dma = pltpu.SemaphoreType.DMA
    out = pl.pallas_call(
        kernel,
        out_shape=jax.ShapeDtypeStruct((2 * NY * NZ, 4, width), jnp.bfloat16),
        in_specs=[
            pl.BlockSpec(memory_space=pltpu.VMEM),
            pl.BlockSpec(memory_space=pltpu.SMEM),
            pl.BlockSpec(memory_space=pltpu.HBM),
        ],
        out_specs=pl.BlockSpec(memory_space=pltpu.VMEM),
        scratch_shapes=[
            pltpu.VMEM((NX, ROWS, 2 * LANES), jnp.bfloat16),
            pltpu.VMEM((NX, ROWS, 2 * LANES), jnp.bfloat16),
            pltpu.VMEM((NY, 2, NZ, ROWS, DATA + LANES), jnp.bfloat16),
            pltpu.VMEM((LANES, depth), jnp.bfloat16),
            pltpu.VMEM((NX, 2 * NZ, ROWS, depth), jnp.bfloat16),
            pltpu.VMEM((NX, depth, width), jnp.bfloat16),
            pltpu.VMEM((32 * NZ, width), jnp.float32),
            dma(()),
            dma((NX - 1,)),
            dma((NX - 1,)),
            dma((NZ,)),
            dma((NZ,)),
            dma((NY - 1, count)),
            dma((NY - 1, count)),
            dma((NY, count)),
            dma((NY, count)),
            dma((2, PARTS + PARTS // 2)),
            dma((2, PARTS + PARTS // 2)),
            pltpu.SemaphoreType.REGULAR((REACH,)),
        ],
        compiler_params=pltpu.CompilerParams(
            collective_id=0, has_side_effects=True, vmem_limit_bytes=62 * 2**20
        ),
    )(amplitudes, pattern, integrals)
    return out


def solution(mesh):
    placed = (P("pair", "red"), P("red", "pair"), P("pair", "red"))
    return jax.shard_map(
        shards, mesh=mesh, in_specs=placed, out_specs=P(None, "red", "pair"), check_vma=False
    )
```

```python
import jax
import jax.numpy as jnp
from jax import lax
from jax.experimental import pallas as pl
from jax.experimental.pallas import tpu as pltpu
from jax.sharding import PartitionSpec as P

MESH = pl.DeviceIdType.MESH
NY, NZ, NX = 4, 16, 4
OFFSETS = (0, 1, -1, 2, -2, 4, -4, 3, -3, 5, -5, 6, -6, 7, -7, 8)
REACH = 4
SLOT = {off % NZ: slot for slot, off in enumerate(OFFSETS)}
PLANE = 1
BATCHES = ((0, 1), (1, 5), (5, 9), (9, 13), (13, 16))
ROWS = 16
BW = 64
LANES = 2 * BW
BLOCKS = 16
KEPT = 8
DATA = KEPT * BW
PARTS = 4


def both_halves(pair):
    low = lax.broadcasted_iota(jnp.int32, pair.shape, 1) < BW
    turned = pltpu.roll(pair, BW, 1)
    return jnp.where(low, pair, turned), jnp.where(low, turned, pair)


def turn(arrays):
    upper = lax.broadcasted_iota(jnp.int32, (8, LANES), 0) < 4
    out = []
    for b in range(4):
        part = [v[8 * (b // 2) : 8 * (b // 2) + 8] for v in arrays]
        if b % 2 == 0:
            halves = [jnp.where(upper, part[i], pltpu.roll(part[i + 1], 4, 0)) for i in (0, 2)]
        else:
            halves = [jnp.where(upper, pltpu.roll(part[i], 4, 0), part[i + 1]) for i in (0, 2)]
        out.append(jnp.concatenate(halves, axis=0))
    return out


def kernel(
    amp_ref, pat_ref, int_ref, out_ref,
    pieces, given, tiles, spread, lhs, slices, total,
    b_sem, xs_sem, xr_sem, zs_sem, zr_sem, ys_sem, yr_sem, cs_sem, cr_sem, bs_sem, br_sem, hello,
):
    pair, r = lax.axis_index("pair"), lax.axis_index("red")
    y, z, c = pair // (2 * NZ), (pair // 2) % NZ, pair % 2
    depth, width = int_ref.shape

    def at_y(d):
        return (((y + d) % NY) * (2 * NZ) + z * 2 + c, r)

    def at_z(d):
        return (y * (2 * NZ) + ((z + d) % NZ) * 2 + c, r)

    def at_x(d):
        return (pair, (r + d) % NX)

    sibling = (pair + 1 - 2 * c, r)

    load_b = pltpu.make_async_copy(int_ref, slices.at[r], b_sem)
    load_b.start()

    barrier = pltpu.get_barrier_semaphore()
    peers = [at_z(-1), at_z(-2)] + [at_y(d) for d in range(1, NY)]
    peers += [at_x(d) for d in range(1, NX)] + [sibling]
    for peer in peers:
        pl.semaphore_signal(barrier, inc=1, device_id=peer, device_id_type=MESH)

    def remote(src, dst, send, recv, device):
        return pltpu.make_async_remote_copy(
            src_ref=src, dst_ref=dst, send_sem=send, recv_sem=recv,
            device_id=device, device_id_type=MESH,
        )

    lane = lax.broadcasted_iota(jnp.int32, (ROWS, LANES), 1)
    row = lax.broadcasted_iota(jnp.int32, (ROWS, LANES), 0)
    place, seen = [], jnp.int32(0)
    for b in range(BLOCKS):
        keep = pat_ref[0, b] > 0
        place.append(jnp.where(keep, seen, 99))
        seen = seen + jnp.where(keep, 1, 0)
    blocks = []
    for j in range(BLOCKS // 2):
        blocks += both_halves(amp_ref[:, LANES * j : LANES * (j + 1)].astype(jnp.float32))
    code = jnp.zeros((ROWS, LANES), jnp.int32)
    for b in range(BLOCKS):
        code = jnp.where(lane == b, place[b], code)
    code = code.astype(jnp.float32).astype(jnp.bfloat16)
    packed = []
    for j in range(KEPT // 2):
        acc = jnp.zeros((ROWS, LANES), jnp.float32)
        for b in range(2 * j, min(BLOCKS, 2 * j + 10)):
            acc = jnp.where(lane // BW + 2 * j == place[b], blocks[b], acc)
        packed.append(acc)
    for d, piece in enumerate(turn(packed)):
        pieces[d, :, :LANES] = piece.astype(jnp.bfloat16)
        pieces[d, :, LANES:] = code
    given[r] = pieces[r]
    wide = lax.broadcasted_iota(jnp.int32, spread.shape, 1) // BW
    spread[...] = jnp.where(
        lax.broadcasted_iota(jnp.int32, spread.shape, 0) == wide, 1.0, 0.0
    ).astype(jnp.bfloat16)

    pl.semaphore_wait(barrier, len(peers))

    def x_copy(d):
        return remote(
            pieces.at[(r + d) % NX], given.at[r], xs_sem.at[d - 1], xr_sem.at[d - 1], at_x(d)
        )

    def z_copy(d):
        slot = SLOT[-d % NZ]
        if abs(d) <= REACH:
            held, device = 0, at_z(d)
        elif abs(d) < 2 * REACH:
            on = REACH if d > 0 else -REACH
            held, device = SLOT[-on % NZ], at_z(d - on)
        else:
            held = jnp.where(c == 0, SLOT[-REACH % NZ], SLOT[REACH])
            device = at_z(REACH - 2 * REACH * c + NZ)
        return remote(
            tiles.at[y, c, held], tiles.at[y, c, slot], zs_sem.at[slot], zr_sem.at[slot], device
        )

    def plane_copy(d):
        slot = SLOT[-d % NZ]
        return remote(
            tiles.at[:, c, 0], tiles.at[:, c, slot], zs_sem.at[slot], zr_sem.at[slot], at_z(d)
        )

    def plane_core_copy(own=True):
        a, b = BATCHES[PLANE]
        part = tiles.at[:, c if own else 1 - c, a:b]
        return remote(part, part, cs_sem.at[0, PLANE], cr_sem.at[0, PLANE], sibling)

    def y_copy(d, k):
        a, b = BATCHES[k]
        part = tiles.at[y, c, a:b]
        return remote(part, part, ys_sem.at[d - 1, k], yr_sem.at[d - 1, k], at_y(d))

    def core_copy(d, k, own=True):
        a, b = BATCHES[k]
        part = tiles.at[(y - d + NY) % NY, c if own else 1 - c, a:b]
        return remote(part, part, cs_sem.at[d, k], cr_sem.at[d, k], sibling)

    rows = depth // PARTS
    half = PARTS // 2

    def own_slice(side, i):
        part = slice(rows * i, rows * (i + 1))
        return remote(
            int_ref.at[part], slices.at[r, part], bs_sem.at[side, i], br_sem.at[side, i], at_x(1 + 2 * side)
        )

    def next_slice(side, i):
        first = rows * (i + half * side)
        part = slices.at[(r + 3 - 2 * side) % NX, first : first + rows]
        return remote(
            part, part, bs_sem.at[side, PARTS + i], br_sem.at[side, PARTS + i], at_x(1 + 2 * side)
        )

    def arrival(side, i):
        if i < PARTS:
            owner, first = (r + 3 - 2 * side) % NX, rows * i
        else:
            owner, first = (r + 2) % NX, rows * (i - PARTS + half * side)
        part = slices.at[owner, first : first + rows]
        return remote(part, part, bs_sem.at[side, i], br_sem.at[side, i], at_x(1 + 2 * side))

    def from_z(k):
        a, b = BATCHES[k]
        if k:
            for slot in range(a, b):
                z_copy(-OFFSETS[slot]).wait_recv()
                if abs(OFFSETS[slot]) == REACH:
                    for more in range(3, 0, -1):
                        z_copy(-OFFSETS[slot] // REACH * (REACH + more)).start()
            if k == 2:
                z_copy(2 * REACH).start()
        for d in (2, 1, 3):
            y_copy(d, k).start()
        core_copy(0, k).start()

    def from_y(k):
        for d in (1, 3, 2):
            y_copy(d, k).wait_recv()
            core_copy(d, k).start()

    def send_on(i):
        for side in range(2):
            arrival(side, i + half * side).wait_recv()
            next_slice(side, i).start()

    def unpack(k):
        a, b = BATCHES[k]
        if k == PLANE:
            plane_core_copy(own=False).wait_recv()
        else:
            for d in range(NY):
                core_copy(d, k, own=False).wait_recv()

        def one(i, _):
            slot, first = a + i // 2, 2 * (i % 2)
            four = [(first + t // 2, t % 2) for t in range(4)]
            places = jnp.concatenate([tiles[yy, cc, slot, :, DATA:] for yy, cc in four], axis=0)
            wanted = jnp.dot(places, spread[...], preferred_element_type=jnp.float32)
            wanted = wanted.astype(jnp.bfloat16)
            kept = []
            for yy, cc in four:
                have = []
                for j in range(KEPT // 2):
                    have += both_halves(
                        tiles[yy, cc, slot, :, LANES * j : LANES * (j + 1)].astype(jnp.float32)
                    )
                kept.append([block.astype(jnp.bfloat16) for block in have])
            for j in range(BLOCKS // 2):
                full = []
                for t in range(4):
                    want = wanted[ROWS * t : ROWS * (t + 1), LANES * j : LANES * (j + 1)]
                    acc = jnp.zeros((ROWS, LANES), jnp.bfloat16)
                    for q in range(max(0, 2 * j - 8), min(KEPT, 2 * j + 2)):
                        acc = jnp.where(want == jnp.bfloat16(q), kept[t][q], acc)
                    full.append(acc.astype(jnp.float32))
                for s, piece in enumerate(turn(full)):
                    lhs[s, 2 * a + i, :, LANES * j : LANES * (j + 1)] = piece.astype(jnp.bfloat16)
            return 0

        lax.fori_loop(0, 2 * (b - a), one, 0)

    def multiply(a, b, distances, add):
        def one(i, _):
            columns = pl.ds(pl.multiple_of(i * (width // 2), width // 2), width // 2)
            value = total[32 * a : 32 * b, columns] if add else None
            for d in distances:
                s = (r + d) % NX
                left = lhs[s, 2 * a : 2 * b].reshape(32 * (b - a), depth)
                term = jnp.dot(left, slices[s, :, columns], preferred_element_type=jnp.float32)
                value = term if value is None else value + term
            total[32 * a : 32 * b, columns] = value
            return 0

        lax.fori_loop(0, 2, one, 0)

    for d in (1, 2):
        pl.semaphore_signal(hello.at[d - 1], inc=1, device_id=at_z(d), device_id_type=MESH)
    for d in (2, 1, 3):
        x_copy(d).start()
    for i in range(PARTS):
        own_slice(0, i).start()
        own_slice(1, (i + half) % PARTS).start()
    for d in range(1, NX):
        came = given.at[(r - d + NX) % NX]
        remote(came, came, xs_sem.at[d - 1], xr_sem.at[d - 1], at_x(d)).wait_recv()
    whole = turn([given[s, :, :LANES].astype(jnp.float32) for s in range(NX)])
    for j in range(KEPT // 2):
        tiles[y, c, 0, :, LANES * j : LANES * (j + 1)] = whole[j].astype(jnp.bfloat16)
    code = jnp.zeros((ROWS, LANES), jnp.float32)
    for s in range(NX):
        code = jnp.where(row // 4 == s, given[s, :, LANES:].astype(jnp.float32), code)
    tiles[y, c, 0, :, DATA:] = code.astype(jnp.bfloat16)

    from_z(0)
    pl.semaphore_wait(hello.at[1], 1)
    pl.semaphore_wait(hello.at[0], 1)
    pl.semaphore_signal(hello.at[2], inc=1, device_id=at_z(-2), device_id_type=MESH)
    pl.semaphore_signal(hello.at[3], inc=1, device_id=at_z(2), device_id_type=MESH)
    pl.semaphore_wait(hello.at[2], 1)
    z_copy(4).start()
    pl.semaphore_wait(hello.at[3], 1)
    for d in (-4, 3, -3):
        z_copy(d).start()
    from_y(0)
    for d in (1, -1, 2, -2):
        plane_copy(d).start()
    from_z(2)
    for d in (1, -1, 2, -2):
        plane_copy(-d).wait_recv()
    plane_core_copy().start()
    from_z(3)
    from_z(4)
    send_on(0)
    from_y(2)
    unpack(0)
    unpack(1)
    from_y(3)
    send_on(1)
    unpack(2)
    from_y(4)
    load_b.wait()
    for i in range(PARTS):
        for side in range(2):
            if i // half != side:
                arrival(side, i).wait_recv()
    multiply(0, BATCHES[2][1], (0, 1, 3), False)
    unpack(3)
    middle, most = BATCHES[2][1], BATCHES[-2][1]
    multiply(middle, most, (0, 1, 3), False)
    unpack(4)
    multiply(most, NZ, (0, 1, 3), False)
    for i in range(half):
        for side in range(2):
            arrival(side, PARTS + i).wait_recv()
    multiply(0, NZ, (2,), True)
    for slot, off in enumerate(OFFSETS):
        result = total[32 * slot : 32 * (slot + 1)].astype(jnp.bfloat16)
        place_in = 2 * ((z + off + NZ) % NZ)
        for yy in range(NY):
            for cc in range(2):
                first = 8 * yy + 4 * cc
                out_ref[2 * NZ * yy + cc + place_in] = result[first : first + 4]

    for d in range(1, NX):
        x_copy(d).wait_send()
    for off in OFFSETS[1:]:
        if abs(off) <= 2:
            plane_copy(off).wait_send()
        else:
            z_copy(off).wait_send()
    plane_core_copy().wait_send()
    for k in range(len(BATCHES)):
        if k == PLANE:
            continue
        for d in range(1, NY):
            y_copy(d, k).wait_send()
        for d in range(NY):
            core_copy(d, k).wait_send()
    for side in range(2):
        for i in range(PARTS):
            own_slice(side, i).wait_send()
        for i in range(half):
            next_slice(side, i).wait_send()


def hand_over(from_ref, to_ref):
    to_ref[...] = from_ref[...]


def shards(amplitudes, integrals, pattern):
    depth, width = integrals.shape
    count = len(BATCHES)
    dma = pltpu.SemaphoreType.DMA
    out = pl.pallas_call(
        kernel,
        out_shape=jax.ShapeDtypeStruct((2 * NY * NZ, 4, width), jnp.bfloat16),
        in_specs=[
            pl.BlockSpec(memory_space=pltpu.VMEM),
            pl.BlockSpec(memory_space=pltpu.SMEM),
            pl.BlockSpec(memory_space=pltpu.HBM),
        ],
        out_specs=pl.BlockSpec(memory_space=pltpu.VMEM),
        scratch_shapes=[
            pltpu.VMEM((NX, ROWS, 2 * LANES), jnp.bfloat16),
            pltpu.VMEM((NX, ROWS, 2 * LANES), jnp.bfloat16),
            pltpu.VMEM((NY, 2, NZ, ROWS, DATA + LANES), jnp.bfloat16),
            pltpu.VMEM((LANES, depth), jnp.bfloat16),
            pltpu.VMEM((NX, 2 * NZ, ROWS, depth), jnp.bfloat16),
            pltpu.VMEM((NX, depth, width), jnp.bfloat16),
            pltpu.VMEM((32 * NZ, width), jnp.float32),
            dma(()),
            dma((NX - 1,)),
            dma((NX - 1,)),
            dma((NZ,)),
            dma((NZ,)),
            dma((NY - 1, count)),
            dma((NY - 1, count)),
            dma((NY, count)),
            dma((NY, count)),
            dma((2, PARTS + PARTS // 2)),
            dma((2, PARTS + PARTS // 2)),
            pltpu.SemaphoreType.REGULAR((REACH,)),
        ],
        compiler_params=pltpu.CompilerParams(
            collective_id=0, has_side_effects=True, vmem_limit_bytes=62 * 2**20
        ),
    )(amplitudes, pattern, integrals)
    return pl.pallas_call(
        hand_over,
        out_shape=jax.ShapeDtypeStruct(out.shape, out.dtype),
        in_specs=[pl.BlockSpec(memory_space=pltpu.VMEM)],
        out_specs=pl.BlockSpec(memory_space=pltpu.VMEM),
    )(out)


def solution(mesh):
    placed = (P("pair", "red"), P("red", "pair"), P("pair", "red"))
    return jax.shard_map(
        shards, mesh=mesh, in_specs=placed, out_specs=P(None, "red", "pair"), check_vma=False
    )
```

```python
import jax
import jax.numpy as jnp
from jax import lax
from jax.experimental import pallas as pl
from jax.experimental.pallas import tpu as pltpu
from jax.sharding import PartitionSpec as P

MESH = pl.DeviceIdType.MESH
NY, NZ, NX = 4, 16, 4
OFFSETS = (0, 1, -1, 2, -2, 4, -4, 3, -3, 5, -5, 6, -6, 7, -7, 8)
REACH = 4
SLOT = {off % NZ: slot for slot, off in enumerate(OFFSETS)}
PLANE = 1
BATCHES = ((0, 1), (1, 5), (5, 9), (9, 13), (13, 16))
ROWS = 16
BW = 64
LANES = 2 * BW
BLOCKS = 16
KEPT = 8
DATA = KEPT * BW
PARTS = 4


def both_halves(pair):
    low = lax.broadcasted_iota(jnp.int32, pair.shape, 1) < BW
    turned = pltpu.roll(pair, BW, 1)
    return jnp.where(low, pair, turned), jnp.where(low, turned, pair)


def turn(arrays):
    upper = lax.broadcasted_iota(jnp.int32, (8, LANES), 0) < 4
    out = []
    for b in range(4):
        part = [v[8 * (b // 2) : 8 * (b // 2) + 8] for v in arrays]
        if b % 2 == 0:
            halves = [jnp.where(upper, part[i], pltpu.roll(part[i + 1], 4, 0)) for i in (0, 2)]
        else:
            halves = [jnp.where(upper, pltpu.roll(part[i], 4, 0), part[i + 1]) for i in (0, 2)]
        out.append(jnp.concatenate(halves, axis=0))
    return out


def kernel(
    amp_ref, pat_ref, int_ref, out_ref,
    pieces, given, tiles, spread, lhs, slices, total,
    b_sem, xs_sem, xr_sem, zs_sem, zr_sem, ys_sem, yr_sem, cs_sem, cr_sem, bs_sem, br_sem, hello,
):
    pair, r = lax.axis_index("pair"), lax.axis_index("red")
    y, z, c = pair // (2 * NZ), (pair // 2) % NZ, pair % 2
    depth, width = int_ref.shape

    def at_y(d):
        return (((y + d) % NY) * (2 * NZ) + z * 2 + c, r)

    def at_z(d):
        return (y * (2 * NZ) + ((z + d) % NZ) * 2 + c, r)

    def at_x(d):
        return (pair, (r + d) % NX)

    sibling = (pair + 1 - 2 * c, r)

    load_b = pltpu.make_async_copy(int_ref, slices.at[r], b_sem)
    load_b.start()

    barrier = pltpu.get_barrier_semaphore()
    peers = [at_z(-1), at_z(-2)] + [at_y(d) for d in range(1, NY)]
    peers += [at_x(d) for d in range(1, NX)] + [sibling]
    for peer in peers:
        pl.semaphore_signal(barrier, inc=1, device_id=peer, device_id_type=MESH)

    def remote(src, dst, send, recv, device):
        return pltpu.make_async_remote_copy(
            src_ref=src, dst_ref=dst, send_sem=send, recv_sem=recv,
            device_id=device, device_id_type=MESH,
        )

    lane = lax.broadcasted_iota(jnp.int32, (ROWS, LANES), 1)
    row = lax.broadcasted_iota(jnp.int32, (ROWS, LANES), 0)
    place, seen = [], jnp.int32(0)
    for b in range(BLOCKS):
        keep = pat_ref[0, b] > 0
        place.append(jnp.where(keep, seen, 99))
        seen = seen + jnp.where(keep, 1, 0)
    blocks = []
    for j in range(BLOCKS // 2):
        blocks += both_halves(amp_ref[:, LANES * j : LANES * (j + 1)].astype(jnp.float32))
    code = jnp.zeros((ROWS, LANES), jnp.int32)
    for b in range(BLOCKS):
        code = jnp.where(lane == b, place[b], code)
    code = code.astype(jnp.float32).astype(jnp.bfloat16)
    packed = []
    for j in range(KEPT // 2):
        acc = jnp.zeros((ROWS, LANES), jnp.float32)
        for b in range(2 * j, min(BLOCKS, 2 * j + 10)):
            acc = jnp.where(lane // BW + 2 * j == place[b], blocks[b], acc)
        packed.append(acc)
    for d, piece in enumerate(turn(packed)):
        pieces[d, :, :LANES] = piece.astype(jnp.bfloat16)
        pieces[d, :, LANES:] = code
    given[r] = pieces[r]
    wide = lax.broadcasted_iota(jnp.int32, spread.shape, 1) // BW
    spread[...] = jnp.where(
        lax.broadcasted_iota(jnp.int32, spread.shape, 0) == wide, 1.0, 0.0
    ).astype(jnp.bfloat16)

    pl.semaphore_wait(barrier, len(peers))

    def x_copy(d):
        return remote(
            pieces.at[(r + d) % NX], given.at[r], xs_sem.at[d - 1], xr_sem.at[d - 1], at_x(d)
        )

    def z_copy(d):
        slot = SLOT[-d % NZ]
        if abs(d) <= REACH:
            held, device = 0, at_z(d)
        elif abs(d) < 2 * REACH:
            on = REACH if d > 0 else -REACH
            held, device = SLOT[-on % NZ], at_z(d - on)
        else:
            held = jnp.where(c == 0, SLOT[-REACH % NZ], SLOT[REACH])
            device = at_z(REACH - 2 * REACH * c + NZ)
        return remote(
            tiles.at[y, c, held], tiles.at[y, c, slot], zs_sem.at[slot], zr_sem.at[slot], device
        )

    def plane_copy(d):
        slot = SLOT[-d % NZ]
        return remote(
            tiles.at[:, c, 0], tiles.at[:, c, slot], zs_sem.at[slot], zr_sem.at[slot], at_z(d)
        )

    def plane_core_copy(own=True):
        a, b = BATCHES[PLANE]
        part = tiles.at[:, c if own else 1 - c, a:b]
        return remote(part, part, cs_sem.at[0, PLANE], cr_sem.at[0, PLANE], sibling)

    def y_copy(d, k):
        a, b = BATCHES[k]
        part = tiles.at[y, c, a:b]
        return remote(part, part, ys_sem.at[d - 1, k], yr_sem.at[d - 1, k], at_y(d))

    def core_copy(d, k, own=True):
        a, b = BATCHES[k]
        part = tiles.at[(y - d + NY) % NY, c if own else 1 - c, a:b]
        return remote(part, part, cs_sem.at[d, k], cr_sem.at[d, k], sibling)

    rows = depth // PARTS
    half = PARTS // 2

    def own_slice(side, i):
        part = slice(rows * i, rows * (i + 1))
        return remote(
            int_ref.at[part], slices.at[r, part], bs_sem.at[side, i], br_sem.at[side, i], at_x(1 + 2 * side)
        )

    def next_slice(side, i):
        first = rows * (i + half * side)
        part = slices.at[(r + 3 - 2 * side) % NX, first : first + rows]
        return remote(
            part, part, bs_sem.at[side, PARTS + i], br_sem.at[side, PARTS + i], at_x(1 + 2 * side)
        )

    def arrival(side, i):
        if i < PARTS:
            owner, first = (r + 3 - 2 * side) % NX, rows * i
        else:
            owner, first = (r + 2) % NX, rows * (i - PARTS + half * side)
        part = slices.at[owner, first : first + rows]
        return remote(part, part, bs_sem.at[side, i], br_sem.at[side, i], at_x(1 + 2 * side))

    def from_z(k):
        a, b = BATCHES[k]
        if k:
            for slot in range(a, b):
                z_copy(-OFFSETS[slot]).wait_recv()
                if abs(OFFSETS[slot]) == REACH:
                    for more in range(3, 0, -1):
                        z_copy(-OFFSETS[slot] // REACH * (REACH + more)).start()
            if k == 2:
                z_copy(2 * REACH).start()
        for d in (2, 1, 3):
            y_copy(d, k).start()
        core_copy(0, k).start()

    def from_y(k):
        for d in (1, 3, 2):
            y_copy(d, k).wait_recv()
            core_copy(d, k).start()

    def send_on(i):
        for side in range(2):
            arrival(side, i + half * side).wait_recv()
            next_slice(side, i).start()

    def unpack(k):
        a, b = BATCHES[k]
        if k == PLANE:
            plane_core_copy(own=False).wait_recv()
        else:
            for d in range(NY):
                core_copy(d, k, own=False).wait_recv()

        def one(i, _):
            slot, first = a + i // 2, 2 * (i % 2)
            four = [(first + t // 2, t % 2) for t in range(4)]
            places = jnp.concatenate([tiles[yy, cc, slot, :, DATA:] for yy, cc in four], axis=0)
            wanted = jnp.dot(places, spread[...], preferred_element_type=jnp.float32)
            wanted = wanted.astype(jnp.bfloat16)
            kept = []
            for yy, cc in four:
                have = []
                for j in range(KEPT // 2):
                    have += both_halves(
                        tiles[yy, cc, slot, :, LANES * j : LANES * (j + 1)].astype(jnp.float32)
                    )
                kept.append([block.astype(jnp.bfloat16) for block in have])
            for j in range(BLOCKS // 2):
                full = []
                for t in range(4):
                    want = wanted[ROWS * t : ROWS * (t + 1), LANES * j : LANES * (j + 1)]
                    acc = jnp.zeros((ROWS, LANES), jnp.bfloat16)
                    for q in range(max(0, 2 * j - 8), min(KEPT, 2 * j + 2)):
                        acc = jnp.where(want == jnp.bfloat16(q), kept[t][q], acc)
                    full.append(acc.astype(jnp.float32))
                for s, piece in enumerate(turn(full)):
                    lhs[s, 2 * a + i, :, LANES * j : LANES * (j + 1)] = piece.astype(jnp.bfloat16)
            return 0

        lax.fori_loop(0, 2 * (b - a), one, 0)

    def multiply(a, b, distances, add):
        def one(i, _):
            columns = pl.ds(pl.multiple_of(i * (width // 2), width // 2), width // 2)
            value = total[32 * a : 32 * b, columns] if add else None
            for d in distances:
                s = (r + d) % NX
                left = lhs[s, 2 * a : 2 * b].reshape(32 * (b - a), depth)
                term = jnp.dot(left, slices[s, :, columns], preferred_element_type=jnp.float32)
                value = term if value is None else value + term
            total[32 * a : 32 * b, columns] = value
            return 0

        lax.fori_loop(0, 2, one, 0)

    for d in (1, 2):
        pl.semaphore_signal(hello.at[d - 1], inc=1, device_id=at_z(d), device_id_type=MESH)
    for d in (2, 1, 3):
        x_copy(d).start()
    for i in range(PARTS):
        own_slice(0, i).start()
        own_slice(1, (i + half) % PARTS).start()
    for d in range(1, NX):
        came = given.at[(r - d + NX) % NX]
        remote(came, came, xs_sem.at[d - 1], xr_sem.at[d - 1], at_x(d)).wait_recv()
    whole = turn([given[s, :, :LANES].astype(jnp.float32) for s in range(NX)])
    for j in range(KEPT // 2):
        tiles[y, c, 0, :, LANES * j : LANES * (j + 1)] = whole[j].astype(jnp.bfloat16)
    code = jnp.zeros((ROWS, LANES), jnp.float32)
    for s in range(NX):
        code = jnp.where(row // 4 == s, given[s, :, LANES:].astype(jnp.float32), code)
    tiles[y, c, 0, :, DATA:] = code.astype(jnp.bfloat16)

    from_z(0)
    pl.semaphore_wait(hello.at[1], 1)
    pl.semaphore_wait(hello.at[0], 1)
    pl.semaphore_signal(hello.at[2], inc=1, device_id=at_z(-2), device_id_type=MESH)
    pl.semaphore_signal(hello.at[3], inc=1, device_id=at_z(2), device_id_type=MESH)
    pl.semaphore_wait(hello.at[2], 1)
    z_copy(4).start()
    pl.semaphore_wait(hello.at[3], 1)
    for d in (-4, 3, -3):
        z_copy(d).start()
    from_y(0)
    for d in (1, -1, 2, -2):
        plane_copy(d).start()
    from_z(2)
    for d in (1, -1, 2, -2):
        plane_copy(-d).wait_recv()
    plane_core_copy().start()
    from_z(3)
    from_z(4)
    send_on(0)
    send_on(1)
    from_y(2)
    unpack(0)
    unpack(1)
    from_y(3)
    unpack(2)
    from_y(4)
    load_b.wait()
    for i in range(PARTS):
        for side in range(2):
            if i // half != side:
                arrival(side, i).wait_recv()
    multiply(0, BATCHES[2][1], (0, 1, 3), False)
    unpack(3)
    middle, most = BATCHES[2][1], BATCHES[-2][1]
    multiply(middle, most, (0, 1, 3), False)
    unpack(4)
    multiply(most, NZ, (0, 1, 3), False)
    for i in range(half):
        for side in range(2):
            arrival(side, PARTS + i).wait_recv()
    multiply(0, NZ, (2,), True)
    for slot, off in enumerate(OFFSETS):
        result = total[32 * slot : 32 * (slot + 1)].astype(jnp.bfloat16)
        place_in = 2 * ((z + off + NZ) % NZ)
        for yy in range(NY):
            for cc in range(2):
                first = 8 * yy + 4 * cc
                out_ref[2 * NZ * yy + cc + place_in] = result[first : first + 4]

    for d in range(1, NX):
        x_copy(d).wait_send()
    for off in OFFSETS[1:]:
        if abs(off) <= 2:
            plane_copy(off).wait_send()
        else:
            z_copy(off).wait_send()
    plane_core_copy().wait_send()
    for k in range(len(BATCHES)):
        if k == PLANE:
            continue
        for d in range(1, NY):
            y_copy(d, k).wait_send()
        for d in range(NY):
            core_copy(d, k).wait_send()
    for side in range(2):
        for i in range(PARTS):
            own_slice(side, i).wait_send()
        for i in range(half):
            next_slice(side, i).wait_send()


def hand_over(from_ref, to_ref):
    to_ref[...] = from_ref[...]


def shards(amplitudes, integrals, pattern):
    depth, width = integrals.shape
    count = len(BATCHES)
    dma = pltpu.SemaphoreType.DMA
    out = pl.pallas_call(
        kernel,
        out_shape=jax.ShapeDtypeStruct((2 * NY * NZ, 4, width), jnp.bfloat16),
        in_specs=[
            pl.BlockSpec(memory_space=pltpu.VMEM),
            pl.BlockSpec(memory_space=pltpu.SMEM),
            pl.BlockSpec(memory_space=pltpu.HBM),
        ],
        out_specs=pl.BlockSpec(memory_space=pltpu.VMEM),
        scratch_shapes=[
            pltpu.VMEM((NX, ROWS, 2 * LANES), jnp.bfloat16),
            pltpu.VMEM((NX, ROWS, 2 * LANES), jnp.bfloat16),
            pltpu.VMEM((NY, 2, NZ, ROWS, DATA + LANES), jnp.bfloat16),
            pltpu.VMEM((LANES, depth), jnp.bfloat16),
            pltpu.VMEM((NX, 2 * NZ, ROWS, depth), jnp.bfloat16),
            pltpu.VMEM((NX, depth, width), jnp.bfloat16),
            pltpu.VMEM((32 * NZ, width), jnp.float32),
            dma(()),
            dma((NX - 1,)),
            dma((NX - 1,)),
            dma((NZ,)),
            dma((NZ,)),
            dma((NY - 1, count)),
            dma((NY - 1, count)),
            dma((NY, count)),
            dma((NY, count)),
            dma((2, PARTS + PARTS // 2)),
            dma((2, PARTS + PARTS // 2)),
            pltpu.SemaphoreType.REGULAR((REACH,)),
        ],
        compiler_params=pltpu.CompilerParams(
            collective_id=0, has_side_effects=True, vmem_limit_bytes=62 * 2**20
        ),
    )(amplitudes, pattern, integrals)
    return pl.pallas_call(
        hand_over,
        out_shape=jax.ShapeDtypeStruct(out.shape, out.dtype),
        in_specs=[pl.BlockSpec(memory_space=pltpu.VMEM)],
        out_specs=pl.BlockSpec(memory_space=pltpu.VMEM),
    )(out)


def solution(mesh):
    placed = (P("pair", "red"), P("red", "pair"), P("pair", "red"))
    return jax.shard_map(
        shards, mesh=mesh, in_specs=placed, out_specs=P(None, "red", "pair"), check_vma=False
    )
```

```python
import jax
import jax.numpy as jnp
from jax import lax
from jax.experimental import pallas as pl
from jax.experimental.pallas import tpu as pltpu
from jax.sharding import PartitionSpec as P

MESH = pl.DeviceIdType.MESH
NY, NZ, NX = 4, 16, 4
OFFSETS = (0, 1, -1, 2, -2, 4, -4, 3, -3, 5, -5, 6, -6, 7, -7, 8)
REACH = 4
SLOT = {off % NZ: slot for slot, off in enumerate(OFFSETS)}
PLANE = 1
BATCHES = ((0, 1), (1, 5), (5, 9), (9, 13), (13, 16))
ROWS = 16
BW = 64
LANES = 2 * BW
BLOCKS = 16
KEPT = 8
DATA = KEPT * BW
PARTS = 4


def both_halves(pair):
    low = lax.broadcasted_iota(jnp.int32, pair.shape, 1) < BW
    turned = pltpu.roll(pair, BW, 1)
    return jnp.where(low, pair, turned), jnp.where(low, turned, pair)


def turn(arrays):
    upper = lax.broadcasted_iota(jnp.int32, (8, LANES), 0) < 4
    out = []
    for b in range(4):
        part = [v[8 * (b // 2) : 8 * (b // 2) + 8] for v in arrays]
        if b % 2 == 0:
            halves = [jnp.where(upper, part[i], pltpu.roll(part[i + 1], 4, 0)) for i in (0, 2)]
        else:
            halves = [jnp.where(upper, pltpu.roll(part[i], 4, 0), part[i + 1]) for i in (0, 2)]
        out.append(jnp.concatenate(halves, axis=0))
    return out


def kernel(
    amp_ref, pat_ref, int_ref, out_ref,
    pieces, given, tiles, spread, lhs, slices, total,
    b_sem, xs_sem, xr_sem, zs_sem, zr_sem, ys_sem, yr_sem, cs_sem, cr_sem, bs_sem, br_sem, hello,
):
    pair, r = lax.axis_index("pair"), lax.axis_index("red")
    y, z, c = pair // (2 * NZ), (pair // 2) % NZ, pair % 2
    depth, width = int_ref.shape

    def at_y(d):
        return (((y + d) % NY) * (2 * NZ) + z * 2 + c, r)

    def at_z(d):
        return (y * (2 * NZ) + ((z + d) % NZ) * 2 + c, r)

    def at_x(d):
        return (pair, (r + d) % NX)

    sibling = (pair + 1 - 2 * c, r)

    load_b = pltpu.make_async_copy(int_ref, slices.at[r], b_sem)
    load_b.start()

    barrier = pltpu.get_barrier_semaphore()
    peers = [at_z(-1), at_z(-2)] + [at_y(d) for d in range(1, NY)]
    peers += [at_x(d) for d in range(1, NX)] + [sibling]
    for peer in peers:
        pl.semaphore_signal(barrier, inc=1, device_id=peer, device_id_type=MESH)

    def remote(src, dst, send, recv, device):
        return pltpu.make_async_remote_copy(
            src_ref=src, dst_ref=dst, send_sem=send, recv_sem=recv,
            device_id=device, device_id_type=MESH,
        )

    lane = lax.broadcasted_iota(jnp.int32, (ROWS, LANES), 1)
    row = lax.broadcasted_iota(jnp.int32, (ROWS, LANES), 0)
    place, seen = [], jnp.int32(0)
    for b in range(BLOCKS):
        keep = pat_ref[0, b] > 0
        place.append(jnp.where(keep, seen, 99))
        seen = seen + jnp.where(keep, 1, 0)
    blocks = []
    for j in range(BLOCKS // 2):
        blocks += both_halves(amp_ref[:, LANES * j : LANES * (j + 1)].astype(jnp.float32))
    code = jnp.zeros((ROWS, LANES), jnp.int32)
    for b in range(BLOCKS):
        code = jnp.where(lane == b, place[b], code)
    code = code.astype(jnp.float32).astype(jnp.bfloat16)
    packed = []
    for j in range(KEPT // 2):
        acc = jnp.zeros((ROWS, LANES), jnp.float32)
        for b in range(2 * j, min(BLOCKS, 2 * j + 10)):
            acc = jnp.where(lane // BW + 2 * j == place[b], blocks[b], acc)
        packed.append(acc)
    for d, piece in enumerate(turn(packed)):
        pieces[d, :, :LANES] = piece.astype(jnp.bfloat16)
        pieces[d, :, LANES:] = code
    given[r] = pieces[r]
    wide = lax.broadcasted_iota(jnp.int32, spread.shape, 1) // BW
    spread[...] = jnp.where(
        lax.broadcasted_iota(jnp.int32, spread.shape, 0) == wide, 1.0, 0.0
    ).astype(jnp.bfloat16)

    pl.semaphore_wait(barrier, len(peers))

    def x_copy(d):
        return remote(
            pieces.at[(r + d) % NX], given.at[r], xs_sem.at[d - 1], xr_sem.at[d - 1], at_x(d)
        )

    def z_copy(d):
        slot = SLOT[-d % NZ]
        if abs(d) <= REACH:
            held, device = 0, at_z(d)
        elif abs(d) < 2 * REACH:
            on = REACH if d > 0 else -REACH
            held, device = SLOT[-on % NZ], at_z(d - on)
        else:
            held = jnp.where(c == 0, SLOT[-REACH % NZ], SLOT[REACH])
            device = at_z(REACH - 2 * REACH * c + NZ)
        return remote(
            tiles.at[y, c, held], tiles.at[y, c, slot], zs_sem.at[slot], zr_sem.at[slot], device
        )

    def plane_copy(d):
        slot = SLOT[-d % NZ]
        return remote(
            tiles.at[:, c, 0], tiles.at[:, c, slot], zs_sem.at[slot], zr_sem.at[slot], at_z(d)
        )

    def plane_core_copy(own=True):
        a, b = BATCHES[PLANE]
        part = tiles.at[:, c if own else 1 - c, a:b]
        return remote(part, part, cs_sem.at[0, PLANE], cr_sem.at[0, PLANE], sibling)

    def y_copy(d, k):
        a, b = BATCHES[k]
        part = tiles.at[y, c, a:b]
        return remote(part, part, ys_sem.at[d - 1, k], yr_sem.at[d - 1, k], at_y(d))

    def core_copy(d, k, own=True):
        a, b = BATCHES[k]
        part = tiles.at[(y - d + NY) % NY, c if own else 1 - c, a:b]
        return remote(part, part, cs_sem.at[d, k], cr_sem.at[d, k], sibling)

    rows = depth // PARTS
    half = PARTS // 2

    def own_slice(side, i):
        part = slice(rows * i, rows * (i + 1))
        return remote(
            int_ref.at[part], slices.at[r, part], bs_sem.at[side, i], br_sem.at[side, i], at_x(1 + 2 * side)
        )

    def next_slice(side, i):
        first = rows * (i + half * side)
        part = slices.at[(r + 3 - 2 * side) % NX, first : first + rows]
        return remote(
            part, part, bs_sem.at[side, PARTS + i], br_sem.at[side, PARTS + i], at_x(1 + 2 * side)
        )

    def arrival(side, i):
        if i < PARTS:
            owner, first = (r + 3 - 2 * side) % NX, rows * i
        else:
            owner, first = (r + 2) % NX, rows * (i - PARTS + half * side)
        part = slices.at[owner, first : first + rows]
        return remote(part, part, bs_sem.at[side, i], br_sem.at[side, i], at_x(1 + 2 * side))

    def from_z(k):
        a, b = BATCHES[k]
        if k:
            for slot in range(a, b):
                z_copy(-OFFSETS[slot]).wait_recv()
                if abs(OFFSETS[slot]) == REACH:
                    for more in range(3, 0, -1):
                        z_copy(-OFFSETS[slot] // REACH * (REACH + more)).start()
            if k == 2:
                z_copy(2 * REACH).start()
        for d in (2, 1, 3):
            y_copy(d, k).start()
        core_copy(0, k).start()

    def from_y(k):
        for d in (1, 3, 2):
            y_copy(d, k).wait_recv()
            core_copy(d, k).start()

    def send_on(i):
        for side in range(2):
            arrival(side, i + half * side).wait_recv()
            next_slice(side, i).start()

    def unpack(k):
        a, b = BATCHES[k]
        if k == PLANE:
            plane_core_copy(own=False).wait_recv()
        else:
            for d in range(NY):
                core_copy(d, k, own=False).wait_recv()

        def one(i, _):
            slot, first = a + i // 2, 2 * (i % 2)
            four = [(first + t // 2, t % 2) for t in range(4)]
            places = jnp.concatenate([tiles[yy, cc, slot, :, DATA:] for yy, cc in four], axis=0)
            wanted = jnp.dot(places, spread[...], preferred_element_type=jnp.float32)
            wanted = wanted.astype(jnp.bfloat16)
            kept = []
            for yy, cc in four:
                have = []
                for j in range(KEPT // 2):
                    have += both_halves(
                        tiles[yy, cc, slot, :, LANES * j : LANES * (j + 1)].astype(jnp.float32)
                    )
                kept.append([block.astype(jnp.bfloat16) for block in have])
            for j in range(BLOCKS // 2):
                full = []
                for t in range(4):
                    want = wanted[ROWS * t : ROWS * (t + 1), LANES * j : LANES * (j + 1)]
                    acc = jnp.zeros((ROWS, LANES), jnp.bfloat16)
                    for q in range(max(0, 2 * j - 8), min(KEPT, 2 * j + 2)):
                        acc = jnp.where(want == jnp.bfloat16(q), kept[t][q], acc)
                    full.append(acc.astype(jnp.float32))
                for s, piece in enumerate(turn(full)):
                    lhs[s, 2 * a + i, :, LANES * j : LANES * (j + 1)] = piece.astype(jnp.bfloat16)
            return 0

        lax.fori_loop(0, 2 * (b - a), one, 0)

    def multiply(a, b, distances, add):
        def one(i, _):
            columns = pl.ds(pl.multiple_of(i * (width // 2), width // 2), width // 2)
            value = total[32 * a : 32 * b, columns] if add else None
            for d in distances:
                s = (r + d) % NX
                left = lhs[s, 2 * a : 2 * b].reshape(32 * (b - a), depth)
                term = jnp.dot(left, slices[s, :, columns], preferred_element_type=jnp.float32)
                value = term if value is None else value + term
            total[32 * a : 32 * b, columns] = value
            return 0

        lax.fori_loop(0, 2, one, 0)

    for d in (1, 2):
        pl.semaphore_signal(hello.at[d - 1], inc=1, device_id=at_z(d), device_id_type=MESH)
    for d in (2, 1, 3):
        x_copy(d).start()
    for i in range(PARTS):
        own_slice(0, i).start()
        own_slice(1, (i + half) % PARTS).start()
    for d in range(1, NX):
        came = given.at[(r - d + NX) % NX]
        remote(came, came, xs_sem.at[d - 1], xr_sem.at[d - 1], at_x(d)).wait_recv()
    whole = turn([given[s, :, :LANES].astype(jnp.float32) for s in range(NX)])
    for j in range(KEPT // 2):
        tiles[y, c, 0, :, LANES * j : LANES * (j + 1)] = whole[j].astype(jnp.bfloat16)
    code = jnp.zeros((ROWS, LANES), jnp.float32)
    for s in range(NX):
        code = jnp.where(row // 4 == s, given[s, :, LANES:].astype(jnp.float32), code)
    tiles[y, c, 0, :, DATA:] = code.astype(jnp.bfloat16)

    from_z(0)
    pl.semaphore_wait(hello.at[1], 1)
    pl.semaphore_wait(hello.at[0], 1)
    pl.semaphore_signal(hello.at[2], inc=1, device_id=at_z(-2), device_id_type=MESH)
    pl.semaphore_signal(hello.at[3], inc=1, device_id=at_z(2), device_id_type=MESH)
    pl.semaphore_wait(hello.at[2], 1)
    z_copy(4).start()
    pl.semaphore_wait(hello.at[3], 1)
    for d in (-4, 3, -3):
        z_copy(d).start()
    from_y(0)
    for d in (1, -1, 2, -2):
        plane_copy(d).start()
    from_z(2)
    for d in (1, -1, 2, -2):
        plane_copy(-d).wait_recv()
    plane_core_copy().start()
    from_z(3)
    from_z(4)
    send_on(0)
    send_on(1)
    from_y(2)
    unpack(0)
    from_y(3)
    unpack(1)
    unpack(2)
    from_y(4)
    load_b.wait()
    for i in range(PARTS):
        for side in range(2):
            if i // half != side:
                arrival(side, i).wait_recv()
    multiply(0, BATCHES[2][1], (0, 1, 3), False)
    unpack(3)
    middle, most = BATCHES[2][1], BATCHES[-2][1]
    multiply(middle, most, (0, 1, 3), False)
    unpack(4)
    multiply(most, NZ, (0, 1, 3), False)
    for i in range(half):
        for side in range(2):
            arrival(side, PARTS + i).wait_recv()
    multiply(0, NZ, (2,), True)
    for slot, off in enumerate(OFFSETS):
        result = total[32 * slot : 32 * (slot + 1)].astype(jnp.bfloat16)
        place_in = 2 * ((z + off + NZ) % NZ)
        for yy in range(NY):
            for cc in range(2):
                first = 8 * yy + 4 * cc
                out_ref[2 * NZ * yy + cc + place_in] = result[first : first + 4]

    for d in range(1, NX):
        x_copy(d).wait_send()
    for off in OFFSETS[1:]:
        if abs(off) <= 2:
            plane_copy(off).wait_send()
        else:
            z_copy(off).wait_send()
    plane_core_copy().wait_send()
    for k in range(len(BATCHES)):
        if k == PLANE:
            continue
        for d in range(1, NY):
            y_copy(d, k).wait_send()
        for d in range(NY):
            core_copy(d, k).wait_send()
    for side in range(2):
        for i in range(PARTS):
            own_slice(side, i).wait_send()
        for i in range(half):
            next_slice(side, i).wait_send()


def hand_over(from_ref, to_ref):
    to_ref[...] = from_ref[...]


def shards(amplitudes, integrals, pattern):
    depth, width = integrals.shape
    count = len(BATCHES)
    dma = pltpu.SemaphoreType.DMA
    out = pl.pallas_call(
        kernel,
        out_shape=jax.ShapeDtypeStruct((2 * NY * NZ, 4, width), jnp.bfloat16),
        in_specs=[
            pl.BlockSpec(memory_space=pltpu.VMEM),
            pl.BlockSpec(memory_space=pltpu.SMEM),
            pl.BlockSpec(memory_space=pltpu.HBM),
        ],
        out_specs=pl.BlockSpec(memory_space=pltpu.VMEM),
        scratch_shapes=[
            pltpu.VMEM((NX, ROWS, 2 * LANES), jnp.bfloat16),
            pltpu.VMEM((NX, ROWS, 2 * LANES), jnp.bfloat16),
            pltpu.VMEM((NY, 2, NZ, ROWS, DATA + LANES), jnp.bfloat16),
            pltpu.VMEM((LANES, depth), jnp.bfloat16),
            pltpu.VMEM((NX, 2 * NZ, ROWS, depth), jnp.bfloat16),
            pltpu.VMEM((NX, depth, width), jnp.bfloat16),
            pltpu.VMEM((32 * NZ, width), jnp.float32),
            dma(()),
            dma((NX - 1,)),
            dma((NX - 1,)),
            dma((NZ,)),
            dma((NZ,)),
            dma((NY - 1, count)),
            dma((NY - 1, count)),
            dma((NY, count)),
            dma((NY, count)),
            dma((2, PARTS + PARTS // 2)),
            dma((2, PARTS + PARTS // 2)),
            pltpu.SemaphoreType.REGULAR((REACH,)),
        ],
        compiler_params=pltpu.CompilerParams(
            collective_id=0, has_side_effects=True, vmem_limit_bytes=62 * 2**20
        ),
    )(amplitudes, pattern, integrals)
    return pl.pallas_call(
        hand_over,
        out_shape=jax.ShapeDtypeStruct(out.shape, out.dtype),
        in_specs=[pl.BlockSpec(memory_space=pltpu.VMEM)],
        out_specs=pl.BlockSpec(memory_space=pltpu.VMEM),
    )(out)


def solution(mesh):
    placed = (P("pair", "red"), P("red", "pair"), P("pair", "red"))
    return jax.shard_map(
        shards, mesh=mesh, in_specs=placed, out_specs=P(None, "red", "pair"), check_vma=False
    )
```
